32 devices in a mesh: dp: 8 (over z, core), tp: 4 (over y, x).
Axes of the slice: x: 2, y: 2, z: 4, core: 2. Of those that a mesh axis runs over, the one named last changes fastest.
Arguments:
- tokens: bfloat16 [4096, 2048], P(('dp', 'tp')), may hold values from -6 to 6
- upstream: bfloat16 [4096, 2048], P(('dp', 'tp')), may hold values from -6 to 6
- segment_ids: int32 [4096], P('dp'), may hold values from 0 to 11, as said below
- positions: int32 [4096], P('dp'), may hold values from 0 to 511, as said below
- norm_gain: float32 [2048], replicated, may hold values from 0.5 to 1.5
- norm_bias: float32 [2048], replicated, may hold values from -3 to 3
- qkv_weight: bfloat16 [2048, 3, 2048], P(None, None, 'tp'), may hold values from -0.125 to 0.125
- qkv_bias: bfloat16 [3, 2048], P(None, 'tp'), may hold values from -3 to 3
- dense_weight: bfloat16 [2048, 2048], P('tp'), may hold values from -0.5 to 0.5
- up_weight: bfloat16 [2048, 8192], P(None, 'tp'), may hold values from -0.125 to 0.125
- up_bias: bfloat16 [8192], P('tp'), may hold values from -3 to 3
- down_weight: bfloat16 [8192, 2048], P('tp'), may hold values from -0.125 to 0.125
- out_bias: float32 [2048], replicated, may hold values from -3 to 3
Outputs:
- mixed: bfloat16 [4096, 2048], P(('dp', 'tp'))
- input_grad: float32 [4096, 2048], P(('dp', 'tp'))
- norm_gain_grad: float32 [2048], replicated
- norm_bias_grad: float32 [2048], replicated
- qkv_weight_grad: float32 [2048, 3, 2048], P(None, None, 'tp')
- qkv_bias_grad: float32 [3, 2048], P(None, 'tp')
- dense_weight_grad: float32 [2048, 2048], P('tp')
- up_weight_grad: float32 [2048, 8192], P(None, 'tp')
- up_bias_grad: float32 [8192], P('tp')
- down_weight_grad: float32 [8192, 2048], P('tp')
- out_bias_grad: float32 [2048], replicated
The draws below stay inside these ranges and needn't reach their ends.
Inputs may be any that keep to these rules, and one draw needn't show every extreme that they name: Each group of 512 tokens on one index of dp holds whole sequences with consecutive segment_ids, rising from group to group; in half of the groups every sequence has 512 tokens, in the other half 256. `positions`: every sequence holds each position from 0 to its length - 1 exactly once.
All inputs are finite; a program needn't handle non-finite values.
Results may differ from the reference program's by a relative error of at most 0.0074.
Values may be sent and summed in bfloat16 or wider, within the bound.
No kernel may reach another device: no remote copies, remote signals or barrier semaphores. Data moves between devices by JAX's collectives and lax.ppermute only.
A program may use at most 256 MiB of HBM per device.

```python
import jax
import jax.numpy as jnp
from jax import lax

D = 2048
HEADS = 32
HEAD_DIM = 64
FF = 8192
ROT = 32
TOK_DEV = 128
LONG_LEN = 512
SHORT_LEN = 256
TOKENS = 4096
N_DP = 8
N_TP = 4


def sequence_layout(key):
    group_rows = TOKENS // N_DP
    group_key, place_key = jax.random.split(key)
    ranking = jax.random.permutation(group_key, N_DP)
    lengths = jnp.where(ranking < N_DP // 2, LONG_LEN, SHORT_LEN).astype(jnp.int32)
    logical = jnp.arange(group_rows, dtype=jnp.int32)
    places = logical[None, :] % lengths[:, None]
    seq_counts = group_rows // lengths
    offsets = jnp.cumsum(seq_counts) - seq_counts
    segments = logical[None, :] // lengths[:, None] + offsets[:, None]
    device_keys = jax.random.split(place_key, N_DP)
    orders = jax.vmap(lambda one_key: jax.random.permutation(one_key, N_TP))(device_keys)
    owners = jnp.take_along_axis(orders, jnp.broadcast_to(logical[None, :] % N_TP, (N_DP, group_rows)), axis=1)
    slots = owners * TOK_DEV + logical[None, :] // N_TP
    row_index = jnp.broadcast_to(jnp.arange(N_DP, dtype=jnp.int32)[:, None], (N_DP, group_rows))
    placed_segments = jnp.zeros((N_DP, group_rows), jnp.int32).at[row_index, slots].set(segments.astype(jnp.int32))
    placed_places = jnp.zeros((N_DP, group_rows), jnp.int32).at[row_index, slots].set(places.astype(jnp.int32))
    return (placed_segments.reshape(-1), placed_places.reshape(-1))


def draw_segment_ids(key, part):
    segments, places = sequence_layout(key)
    return segments


def draw_positions(key, part):
    segments, places = sequence_layout(key)
    return places


def block_scale(key, shape, pieces, low, largest):
    factor_of = 1.0
    for dim, shards_of in pieces:
        draws = jax.random.uniform(jax.random.fold_in(jax.random.fold_in(key, 6), dim), (shards_of,), jnp.float32, low / len(pieces), largest / len(pieces))
        factor_of = factor_of * jnp.repeat(jnp.exp(draws), shape[dim] // shards_of).reshape((-1,) + (1,) * (len(shape) - 1 - dim))
    return factor_of


def noise(own_key, extent, scale, reach, shards=(), kind=jnp.bfloat16):
    factor_of = block_scale(own_key, extent, shards, -0.22, 0.18) if shards else 1.0
    result = jax.random.normal(own_key, extent, jnp.float32) * scale * factor_of
    return jnp.minimum(jnp.maximum(result, -reach), reach).astype(kind)


def setup_inputs(seed: int = 0) -> dict:
    streams_of = jax.random.split(jax.random.key(seed), 14)
    tokens = noise(streams_of[0], (TOKENS, D), 1.0, 6.0, ((0, 32),))
    upstream = noise(streams_of[1], (TOKENS, D), 1.0, 6.0, ((0, 32),))
    segment_ids = draw_segment_ids(jax.random.fold_in(streams_of[13], 71), 0)
    positions = draw_positions(jax.random.fold_in(streams_of[13], 71), 0)
    norm_gain = jnp.clip(1.0 + 0.1 * jax.random.normal(streams_of[4], (D,), jnp.float32), 0.5, 1.5)
    norm_bias = noise(streams_of[5], (D,), 0.3, 3.0, (), jnp.float32)
    qkv_weight = noise(streams_of[6], (D, 3, D), D ** -0.5, 0.125, ((2, 4),))
    qkv_bias = noise(streams_of[7], (3, D), 0.5, 3.0, ((1, 4),))
    dense_weight = noise(streams_of[8], (D, D), (D // 16) ** -0.5, 0.5, ((0, 4),))
    up_weight = noise(streams_of[9], (D, FF), D ** -0.5, 0.125, ((1, 4),))
    up_bias = noise(streams_of[10], (FF,), 0.5, 3.0, ((0, 4),))
    down_weight = noise(streams_of[11], (FF, D), (FF // 4) ** -0.5, 0.125, ((0, 4),))
    out_bias = noise(streams_of[12], (D,), 0.5, 3.0, (), jnp.float32)
    return {"tokens": tokens, "upstream": upstream, "segment_ids": segment_ids, "positions": positions, "norm_gain": norm_gain, "norm_bias": norm_bias, "qkv_weight": qkv_weight, "qkv_bias": qkv_bias, "dense_weight": dense_weight, "up_weight": up_weight, "up_bias": up_bias, "down_weight": down_weight, "out_bias": out_bias}


highest = lax.Precision.HIGHEST
norm_epsilon = 1e-05
masked_score = -1e+30

@jax.custom_vjp
def low(v):
    return lax.optimization_barrier(v.astype(jnp.bfloat16)).astype(jnp.float32)

@jax.custom_vjp
def low_back(v):
    return v

def low_keep(v):
    return (low(v), None)

def low_pass(kept, grad):
    return (grad,)

def back_keep(v):
    return (v, None)

def back_low(kept, grad):
    return (low(grad),)
low.defvjp(low_keep, low_pass)
low_back.defvjp(back_keep, back_low)

def layer_norm(values, gain, shift):
    averaged = lax.optimization_barrier(jnp.mean(values, -1, keepdims=True))
    centred = values - averaged
    spread = lax.optimization_barrier(jnp.mean(centred * centred, -1, keepdims=True))
    return centred * lax.rsqrt(spread + norm_epsilon) * gain + shift

def rotary_tables(places, rot_dims):
    half_rot = rot_dims // 2
    frequency = jnp.power(10000.0, -2.0 * jnp.arange(half_rot).astype(jnp.float32) / rot_dims)
    phases = places.astype(jnp.float32)[:, None] * frequency[None, :]
    cosine_table = jnp.concatenate([jnp.cos(phases), jnp.cos(phases)], -1)[:, None, :]
    sine_table = jnp.concatenate([jnp.sin(phases), jnp.sin(phases)], -1)[:, None, :]
    return (cosine_table, sine_table)

def rotate(values, cosine_table, sine_table):
    rot_dims = cosine_table.shape[-1]
    half_rot = rot_dims // 2
    rotated_part = values[..., :rot_dims]
    turned = jnp.concatenate([-rotated_part[..., half_rot:], rotated_part[..., :half_rot]], -1)
    return jnp.concatenate([rotated_part * cosine_table + turned * sine_table, values[..., rot_dims:]], -1)

def group_block(inputs, seg_group, place_group, weights):
    norm_gain, norm_bias, qkv_weight, qkv_bias, dense_weight, up_weight, up_bias, down_weight, out_bias = weights
    group_rows = inputs.shape[0]
    normed = low(layer_norm(inputs, norm_gain, norm_bias))
    projected = low_back(jnp.einsum('td,dch->tch', normed, qkv_weight, precision=highest) + qkv_bias[None])
    head_shape = (group_rows, HEADS, HEAD_DIM)
    cosine_table, sine_table = rotary_tables(place_group, ROT)
    queries = low(rotate(projected[:, 0].reshape(head_shape), cosine_table, sine_table))
    keys_all = low(rotate(projected[:, 1].reshape(head_shape), cosine_table, sine_table))
    values_all = low(projected[:, 2].reshape(head_shape))
    allowed = (seg_group[:, None] == seg_group[None, :]) & (place_group[None, :] <= place_group[:, None])

    def one_head(operands):
        query_head, key_head, value_head = operands
        scores = low_back(jnp.dot(query_head, key_head.T, precision=highest) * 0.125)
        scores = jnp.where(allowed, scores, masked_score)
        attn_soft = jax.nn.softmax(scores, axis=-1)
        return jnp.dot(low(attn_soft), value_head, precision=highest)
    context = lax.map(jax.checkpoint(one_head), (queries.transpose(1, 0, 2), keys_all.transpose(1, 0, 2), values_all.transpose(1, 0, 2)))
    context = low_back(low(context.transpose(1, 0, 2).reshape(group_rows, HEADS * HEAD_DIM)))
    attended = jnp.dot(context, dense_weight, precision=highest)
    up_input = low_back(jnp.dot(normed, up_weight, precision=highest) + up_bias)
    up_active = low(jax.nn.gelu(up_input, approximate=True))
    return inputs + attended + jnp.dot(up_active, down_weight, precision=highest) + out_bias

def reference(tokens, upstream, segment_ids, positions, norm_gain, norm_bias, qkv_weight, qkv_bias, dense_weight, up_weight, up_bias, down_weight, out_bias):
    params = (norm_gain.astype(jnp.float32), norm_bias.astype(jnp.float32), qkv_weight.astype(jnp.float32), qkv_bias.astype(jnp.float32), dense_weight.astype(jnp.float32), up_weight.astype(jnp.float32), up_bias.astype(jnp.float32), down_weight.astype(jnp.float32), out_bias.astype(jnp.float32))
    group_rows = TOKENS // N_DP
    seg_groups = segment_ids.reshape(N_DP, group_rows)
    place_groups = positions.reshape(N_DP, group_rows)
    checked = jax.checkpoint(group_block)

    def whole(inputs, weights):

        def step(running, operands):
            return (running, checked(operands[0], operands[1], operands[2], weights))
        _, outputs = lax.scan(step, None, (inputs.reshape(N_DP, group_rows, D), seg_groups, place_groups))
        return outputs.reshape(TOKENS, D)
    mixed, pullback = jax.vjp(whole, tokens.astype(jnp.float32), params)
    input_grad, grads = pullback(upstream.astype(jnp.float32))
    return (mixed.astype(jnp.bfloat16), input_grad, grads[0], grads[1], grads[2], grads[3], grads[4], grads[5], grads[6], grads[7], grads[8])
```

```python
from functools import partial
import math

import jax
import jax.numpy as jnp
from jax import lax
from jax.experimental import pallas as pl
from jax.experimental.pallas import tpu as pltpu
from jax.sharding import PartitionSpec as P

HEAD_DIM = 64
ROT = 32
norm_epsilon = 1e-05
masked_score = -1e30
low = jnp.bfloat16
wide = jnp.float32
VMEM = 56 * 2**20
HASTE = 0.1


def dot(left, right, left_dim, right_dim, kind=wide):
    return lax.dot_general(
        left, right, (((left_dim,), (right_dim,)), ((), ())), preferred_element_type=wide
    ).astype(kind)


def layer_norm(values, gain, shift):
    averaged = jnp.mean(values, -1, keepdims=True)
    centred = values - averaged
    spread = jnp.mean(centred * centred, -1, keepdims=True)
    return centred * lax.rsqrt(spread + norm_epsilon) * gain + shift


def rotary_tables(places, rot_dims):
    half_rot = rot_dims // 2
    frequency = jnp.power(10000.0, -2.0 * jnp.arange(half_rot).astype(wide) / rot_dims)
    phases = places.astype(wide)[:, None] * frequency[None, :]
    cosine_table = jnp.concatenate([jnp.cos(phases), jnp.cos(phases)], -1)[:, None, :]
    sine_table = jnp.concatenate([jnp.sin(phases), jnp.sin(phases)], -1)[:, None, :]
    return (cosine_table, sine_table)


def rotate(values, cosine_table, sine_table):
    rot_dims = cosine_table.shape[-1]
    half_rot = rot_dims // 2
    rotated_part = values[..., :rot_dims]
    turned = jnp.concatenate([-rotated_part[..., half_rot:], rotated_part[..., :half_rot]], -1)
    return jnp.concatenate(
        [rotated_part * cosine_table + turned * sine_table, values[..., rot_dims:]], -1
    )


def gelu_and_slope(v):
    inner = jnp.tanh(0.7978845608 * (v + 0.044715 * v * v * v))
    half = 0.5 * (1.0 + inner)
    slope = half + 0.5 * v * (1.0 - inner * inner) * 0.7978845608 * (1.0 + 0.134145 * v * v)
    return v * half, slope


def kernel_call(body, flops, out_shape, **kinds):
    return pl.pallas_call(
        body,
        out_shape=out_shape,
        compiler_params=pltpu.CompilerParams(vmem_limit_bytes=VMEM),
        cost_estimate=pl.CostEstimate(
            flops=int(flops * HASTE), bytes_accessed=int(flops * HASTE) // 512, transcendentals=0
        ),
        **kinds,
    )


def sds(shape, kind):
    return jax.ShapeDtypeStruct(shape, kind)


def whole_block(array):
    zeros = (0,) * array.ndim
    return pl.BlockSpec(array.shape, lambda *_: zeros, pipeline_mode=pl.Buffered(1))


def fixed_block(shape):
    zeros = (0,) * len(shape)
    return pl.BlockSpec(shape, lambda *_: zeros)


def assemble(target, pieces):
    at = 0
    for ref, first, size in pieces:
        target[at : at + size, :] = ref[first : first + size, :]
        at += size


def turned(values, cosine, sine_low, sine_high):
    return (
        values * cosine
        + pltpu.roll(values, 128 - ROT // 2, 1) * sine_low
        + pltpu.roll(values, ROT // 2, 1) * sine_high
    )


def row_means(inputs):
    centred = inputs - jnp.mean(inputs, -1, keepdims=True)
    spread = jnp.mean(centred * centred, -1, keepdims=True)
    scale = lax.rsqrt(spread + norm_epsilon)
    return centred * scale, scale


def norm_kernel(tokens, upstream, gain, shift, normed, both):
    unit, _ = row_means(tokens[...].astype(wide))
    rows = tokens.shape[0]
    normed[...] = (unit * gain[...] + shift[...]).astype(low)
    both[:rows, :] = normed[...]
    both[rows:, :] = upstream[...]


def norm_rows(tokens, upstream, gain, shift):
    rows, features = tokens.shape
    arrays = [tokens, upstream, gain, shift]
    return kernel_call(
        norm_kernel,
        rows * features * 512,
        [sds((rows, features), low), sds((2 * rows, features), low)],
        grid=(1,),
        in_specs=[whole_block(a) for a in arrays],
        out_specs=[fixed_block((rows, features)), fixed_block((2 * rows, features))],
    )(*arrays)


def norm_back_kernel(tokens, upstream, gain, out_bias, own, got_1, got_2, got_3, mixed, input_grad, sums):
    rows = tokens.shape[0]
    inputs, cotangent = tokens[...].astype(wide), upstream[...].astype(wide)

    def total(first):
        span = slice(first, first + rows)
        return (own[span, :] + got_1[span, :].astype(wide)) + (
            got_2[span, :].astype(wide) + got_3[span, :].astype(wide)
        )

    mixed[...] = (inputs + total(0) + out_bias[...]).astype(low)
    unit, scale = row_means(inputs)
    normed_grad = total(rows)
    e = normed_grad * gain[...]
    along = jnp.mean(e * unit, -1, keepdims=True)
    input_grad[...] = cotangent + (e - jnp.mean(e, -1, keepdims=True) - unit * along) * scale
    sums[0:1, :] = jnp.sum(normed_grad * unit, 0, keepdims=True)
    sums[1:2, :] = jnp.sum(normed_grad, 0, keepdims=True)
    sums[2:3, :] = jnp.sum(cotangent, 0, keepdims=True)


def norm_back(*arrays):
    rows, features = arrays[0].shape
    shapes = [(rows, features), (rows, features), (3, features)]
    return kernel_call(
        norm_back_kernel,
        rows * features * 1024,
        [sds(s, k) for s, k in zip(shapes, (low, wide, wide))],
        grid=(1,),
        in_specs=[whole_block(a) for a in arrays],
        out_specs=[fixed_block(s) for s in shapes],
    )(*arrays)


def project_kernel(count, *refs):
    weight, bias, cosine, sine_low, sine_high, rows_out, out = refs[count:]
    part = pl.program_id(0)

    @pl.when(part == 0)
    def _():
        assemble(rows_out, [(r, 0, r.shape[0]) for r in refs[:count]])

    projected = dot(rows_out[...], weight[0], 1, 0) + bias[0].astype(wide)

    @pl.when(part < 2)
    def _():
        scale = jnp.where(part == 0, 0.125, 1.0)
        for j in range(0, projected.shape[1], 128):
            rotated = turned(projected[:, j : j + 128], cosine[...], sine_low[...], sine_high[...])
            out[0, :, j : j + 128] = (rotated * scale).astype(low)

    @pl.when(part == 2)
    def _():
        out[0] = projected.astype(low)


def project(blocks, weight, bias, tables):
    tokens = sum(b.shape[0] for b in blocks)
    _, features, width = weight.shape
    table = whole_block(tables[0])
    return kernel_call(
        partial(project_kernel, len(blocks)),
        6 * tokens * features * width,
        [sds((tokens, features), low), sds((3, tokens, width), low)],
        grid=(3,),
        in_specs=[whole_block(a) for a in blocks]
        + [
            pl.BlockSpec((1, features, width), lambda c: (c, 0, 0)),
            pl.BlockSpec((1, 1, width), lambda c: (c, 0, 0)),
            table,
            table,
            table,
        ],
        out_specs=[fixed_block((tokens, features)), pl.BlockSpec((1, tokens, width), lambda c: (c, 0, 0))],
    )(*blocks, weight, bias, *tables)


def attention_kernel(count, *refs):
    (queries, keys, values, dense, seg_q, place_q, seg_k, place_k, cosine, sine_low, sine_high) = refs[count:-5]
    rows_out, context, out, bias_out, mask = refs[-5:]

    @pl.when(pl.program_id(0) == 0)
    def _():
        assemble(rows_out, [(r, 0, r.shape[0]) for r in refs[:count]])
        allowed = (seg_q[...] == seg_k[...]) & (place_k[...] <= place_q[...])
        mask[...] = jnp.where(allowed, 0.0, masked_score)

    q, k, v = queries[0], keys[0], values[0]
    g = dot(rows_out[...], dense[...], 1, 1, low)
    lane = lax.broadcasted_iota(jnp.int32, q.shape, 1) // HEAD_DIM
    found = []
    for head in range(128 // HEAD_DIM):
        mine = lane == head
        scores = dot(jnp.where(mine, q, jnp.zeros_like(q)), k, 1, 1) + mask[...]
        exponent = jnp.exp(scores - jnp.max(scores, -1, keepdims=True))
        soft = exponent * (1.0 / jnp.sum(exponent, -1, keepdims=True))
        soft_low = soft.astype(low)
        prob_grad = dot(jnp.where(mine, g, jnp.zeros_like(g)), v, 1, 1)
        row_dots = jnp.sum(soft * prob_grad, -1, keepdims=True)
        score_grad = (soft * (prob_grad - row_dots)).astype(low)
        found.append(
            (dot(soft_low, v, 1, 0), dot(score_grad, k, 1, 0), dot(score_grad, q, 0, 0), dot(soft_low, g, 0, 0))
        )
    parts = [jnp.where(lane == 0, a, b) for a, b in zip(*found)]
    context[...] = parts[0].astype(low)
    back = (cosine[...], -sine_low[...], -sine_high[...])
    grads = [turned(parts[1] * 0.125, *back), turned(parts[2], *back), parts[3]]
    for c, value in enumerate(grads):
        rounded = value.astype(low)
        out[c] = rounded
        bias_out[c] = jnp.sum(rounded.astype(wide), 0, keepdims=True)


def attention(blocks, qkv, dense_weight, seg, place, tables):
    _, tokens, width = qkv.shape
    features = dense_weight.shape[1]
    column, row = (lambda a: a.reshape(tokens, 1)), (lambda a: a.reshape(1, tokens))
    extras = [column(seg), column(place), row(seg), row(place), *tables]
    part = lambda c: pl.BlockSpec((1, tokens, 128), lambda j: (c, 0, j))
    return kernel_call(
        partial(attention_kernel, len(blocks)),
        20 * tokens * tokens * width,
        [
            sds((tokens, features), low),
            sds((tokens, width), low),
            sds((3, tokens, width), low),
            sds((3, 1, width), wide),
        ],
        grid=(width // 128,),
        in_specs=[whole_block(b) for b in blocks]
        + [part(0), part(1), part(2), pl.BlockSpec((128, features), lambda j: (j, 0))]
        + [whole_block(e) for e in extras],
        out_specs=[
            fixed_block((tokens, features)),
            pl.BlockSpec((tokens, 128), lambda j: (0, j)),
            pl.BlockSpec((3, tokens, 128), lambda j: (0, 0, j)),
            pl.BlockSpec((3, 1, 128), lambda j: (0, 0, j)),
        ],
        scratch_shapes=[pltpu.VMEM((tokens, tokens), wide)],
    )(*blocks, qkv, qkv, qkv, dense_weight, *extras)


def outer_parts_kernel(left, right, out):
    out[0] = dot(left[...], right[0], 0, 0, low)


def outer_parts(left, right, tile=1024):
    count, tokens, n = right.shape
    m = left.shape[1]
    return kernel_call(
        outer_parts_kernel,
        2 * count * tokens * m * n,
        sds((count, m, n), low),
        grid=(m // tile, count),
        in_specs=[
            pl.BlockSpec((tokens, tile), lambda i, c: (0, i)),
            pl.BlockSpec((1, tokens, n), lambda i, c: (c, 0, 0)),
        ],
        out_specs=pl.BlockSpec((1, tile, n), lambda i, c: (c, i, 0)),
    )(left, right)


def feed_kernel(layouts, n_arrays, *refs):
    arrays, refs = refs[:n_arrays], refs[n_arrays:]
    up_weight, down_weight, up_bias = refs[:3]
    outs = refs[3:]
    pick = lambda layout: [(arrays[i], first, size) for i, first, size in layout]

    @pl.when(pl.program_id(0) == 0)
    def _():
        for (normed_layout, upstream_layout), (normed_out, upstream_out, *_) in zip(layouts, fives(outs)):
            assemble(normed_out, pick(normed_layout))
            assemble(upstream_out, pick(upstream_layout))

    bias = up_bias[...].astype(wide)
    for normed_out, upstream_out, active_out, grad_out, sum_out in fives(outs):
        active, slope = gelu_and_slope(dot(normed_out[...], up_weight[...], 1, 0) + bias)
        active_out[...] = active.astype(low)
        rounded = (dot(upstream_out[...], down_weight[...], 1, 1) * slope).astype(low)
        grad_out[...] = rounded
        sum_out[...] = jnp.sum(rounded.astype(wide), 0, keepdims=True)


def fives(outs):
    return [outs[i : i + 5] for i in range(0, len(outs), 5)]


def feed(arrays, layouts, up_weight, down_weight, up_bias, tile=512):
    features, hidden = up_weight.shape
    tokens = sum(size for _, _, size in layouts[0][0])
    rows_spec = fixed_block((tokens, features))
    tile_spec = pl.BlockSpec((tokens, tile), lambda j: (0, j))
    sum_spec = pl.BlockSpec((1, tile), lambda j: (0, j))
    shapes = [sds((tokens, features), low)] * 2 + [sds((tokens, hidden), low)] * 2 + [sds((1, hidden), wide)]
    found = kernel_call(
        partial(feed_kernel, layouts, len(arrays)),
        4 * len(layouts) * tokens * features * hidden,
        shapes * len(layouts),
        grid=(hidden // tile,),
        in_specs=[whole_block(a) for a in arrays]
        + [
            pl.BlockSpec((features, tile), lambda j: (0, j)),
            pl.BlockSpec((tile, features), lambda j: (j, 0)),
            pl.BlockSpec((1, tile), lambda j: (0, j)),
        ],
        out_specs=[rows_spec, rows_spec, tile_spec, tile_spec, sum_spec] * len(layouts),
    )(*arrays, up_weight, down_weight, up_bias)
    return fives(found)


def back_kernel(n_tp, active, context, up_grad, part_grad, down, dense, up, part_weight, own, *sent):
    rows = active.shape[0] // n_tp
    mixed = dot(active[...], down[...], 1, 0) + dot(context[...], dense[...], 1, 0)
    normed_grad = dot(up_grad[...], up[...], 1, 1)
    for c in range(3):
        normed_grad = normed_grad + dot(part_grad[c], part_weight[c], 1, 1)
    for i, value in enumerate((mixed, normed_grad)):
        span = slice(i * rows, (i + 1) * rows)
        own[span, :] = value[:rows]
        for r in range(1, n_tp):
            sent[r - 1][span, :] = value[r * rows : (r + 1) * rows].astype(low)


def back_to_tokens(n_tp, active, context, up_grad, part_grad, down, dense, up, part_weight, tile=512):
    tokens, hidden = active.shape
    features, width = down.shape[1], context.shape[1]
    rows = 2 * tokens // n_tp
    column = pl.BlockSpec((rows, tile), lambda j: (0, j))
    return kernel_call(
        partial(back_kernel, n_tp),
        4 * tokens * features * (hidden + 2 * width),
        [sds((rows, features), wide)] + [sds((rows, features), low)] * (n_tp - 1),
        grid=(features // tile,),
        in_specs=[whole_block(a) for a in (active, context, up_grad, part_grad)]
        + [
            pl.BlockSpec((hidden, tile), lambda j: (0, j)),
            pl.BlockSpec((width, tile), lambda j: (0, j)),
            pl.BlockSpec((tile, hidden), lambda j: (j, 0)),
            pl.BlockSpec((3, tile, width), lambda j: (0, j, 0)),
        ],
        out_specs=[column] * n_tp,
    )(active, context, up_grad, part_grad, down, dense, up, part_weight)


def outer_kernel(count, place, *refs):
    out = refs[2 * count]
    for here in range(count):

        @pl.when(place[0] == here)
        def _():
            total = None
            for there in range(count):
                i = here ^ there
                term = dot(refs[i][...], refs[count + i][...], 0, 0)
                total = term if total is None else total + term
            out[...] = total.astype(out.dtype)


def outer_sum(place, lefts, rights, tile_m=512, tile_n=1024):
    count, (tokens, m), n = len(lefts), lefts[0].shape, rights[0].shape[1]
    return kernel_call(
        partial(outer_kernel, count),
        2 * count * tokens * m * n,
        sds((m, n), low),
        grid_spec=pltpu.PrefetchScalarGridSpec(
            num_scalar_prefetch=1,
            grid=(n // tile_n, m // tile_m),
            in_specs=[pl.BlockSpec((tokens, tile_m), lambda j, i, _: (0, i))] * count
            + [pl.BlockSpec((tokens, tile_n), lambda j, i, _: (0, j))] * count,
            out_specs=pl.BlockSpec((tile_m, tile_n), lambda j, i, _: (i, j)),
        ),
    )(place.reshape(1).astype(jnp.int32), *lefts, *rights)


def add_kernel(*refs):
    total = refs[0][...].astype(wide)
    for ref in refs[1:-1]:
        total = total + ref[...].astype(wide)
    refs[-1][...] = total


def added(*terms, tile=512):
    m, n = terms[0].shape
    spec = pl.BlockSpec((tile, n), lambda i: (i, 0))
    return kernel_call(
        add_kernel, m * n * 256, sds((m, n), wide), grid=(m // tile,), in_specs=[spec] * len(terms), out_specs=spec
    )(*terms)


def tie(*arrays):
    return lax.optimization_barrier(arrays)


def shards(
    tokens,
    upstream,
    segment_ids,
    positions,
    norm_gain,
    norm_bias,
    qkv_weight,
    qkv_bias,
    dense_weight,
    up_weight,
    up_bias,
    down_weight,
    out_bias,
):
    n_tp, n_line = 4, 4
    dp_place, tp_place = lax.axis_index("dp"), lax.axis_index("tp")
    line_place = dp_place // 2
    rows, features = tokens.shape
    group_rows = rows * n_tp
    heads_wide = qkv_weight.shape[2]
    hidden = up_weight.shape[1]

    def swap_tp(array, flip):
        return lax.ppermute(array, "tp", [(i, i ^ flip) for i in range(n_tp)])

    def swap_core(array):
        return lax.ppermute(array, "dp", [(i, i ^ 1) for i in range(2 * n_line)])

    def swap_line(array, flip):
        return lax.ppermute(array, "dp", [(i, i ^ (2 * flip)) for i in range(2 * n_line)])

    def hop(array, pairs):
        return lax.ppermute(array, "dp", [(2 * s + c, 2 * d + c) for s, d in pairs for c in (0, 1)])

    def from_others(array):
        return [swap_tp(array, r) for r in range(1, n_tp)]

    gain, shift, last_bias = (a.reshape(1, features) for a in (norm_gain, norm_bias, out_bias))
    normed, both = norm_rows(tokens, upstream, gain, shift)
    normed_blocks = [normed, *from_others(normed)]
    above_1, below_1 = hop(both, [(0, 1), (1, 2), (2, 3)]), hop(both, [(1, 0), (2, 1), (3, 2)])

    by_owner = jnp.stack([segment_ids.reshape(n_tp, rows), positions.reshape(n_tp, rows)])
    owner = tp_place ^ jnp.arange(n_tp)
    pick = (owner[:, None] == jnp.arange(n_tp)[None, :]).astype(jnp.int32)
    arranged = jnp.sum(pick[None, :, :, None] * by_owner[:, None, :, :], 2).reshape(2, group_rows)
    seg, place = arranged[0], arranged[1]
    cosine_table, sine_table = rotary_tables(place, ROT)
    cosine, sine = cosine_table[:, 0, :], sine_table[:, 0, :]
    still = jnp.zeros((group_rows, HEAD_DIM - ROT), wide)
    quiet = jnp.zeros((group_rows, ROT // 2), wide)
    tables = [
        jnp.concatenate([cosine, still + 1.0], 1),
        jnp.concatenate([-sine[:, : ROT // 2], quiet, still], 1),
        jnp.concatenate([quiet, sine[:, : ROT // 2], still], 1),
    ]
    tables = [jnp.concatenate([t] * (128 // HEAD_DIM), 1) for t in tables]
    parts_weight = qkv_weight.transpose(1, 0, 2)
    parts_bias = qkv_bias.reshape(3, 1, heads_wide)

    normed_blocks, tables, late_upstream, seg, place, above_1, below_1 = tie(
        normed_blocks, tables, upstream, seg, place, above_1, below_1
    )
    above_2, below_2 = hop(above_1, [(1, 2), (2, 3)]), hop(below_1, [(1, 0), (2, 1)])
    slot_1 = jnp.where(line_place % 2 == 1, above_1, below_1)
    upstream_blocks = [late_upstream, *from_others(late_upstream)]
    group_normed, qkv = project(normed_blocks, parts_weight, parts_bias, tables)

    upstream_blocks, slot_1, above_2, below_2, group_normed, qkv = tie(
        upstream_blocks, slot_1, above_2, below_2, group_normed, qkv
    )
    above_3, below_3 = hop(above_2, [(2, 3)]), hop(below_2, [(1, 0)])
    slot_2 = jnp.where(line_place >= 2, above_2, below_2)
    slot_1 = [slot_1, *from_others(slot_1)]
    group_upstream, context, projected_grad, qkv_bias_grad = attention(
        upstream_blocks, qkv, dense_weight, seg, place, tables
    )
    qkv_part = outer_parts(group_normed, projected_grad)
    dense_part = outer_sum(0 * line_place, [context], [group_upstream], heads_wide, features // 2)
    qkv_sum, dense_sum = lax.psum((qkv_part, dense_part), "dp")

    slot_layout = (
        [(i, 0, rows) for i in range(n_tp)],
        [(i, rows, rows) for i in range(n_tp)],
    )
    weights = (up_weight, down_weight, up_bias.reshape(1, hidden))
    slot_3 = jnp.where(
        line_place == 0, below_3, jnp.where(line_place == 1, below_1, jnp.where(line_place == 2, above_1, above_3))
    )
    slot_1, slot_2, slot_3, group_upstream, context, projected_grad, _, _ = tie(
        slot_1, slot_2, slot_3, group_upstream, context, projected_grad, qkv_part, dense_part
    )
    slot_2 = [slot_2, *from_others(slot_2)]
    own_layout = ([(n_tp, 0, group_rows)], [(n_tp + 1, 0, group_rows)])
    group_1, group_0 = feed([*slot_1, group_normed, group_upstream], [slot_layout, own_layout], *weights)
    slot_2, slot_3, group_0, group_1 = tie(slot_2, slot_3, group_0, group_1)
    slot_3 = [slot_3, *from_others(slot_3)]
    active, up_input_grad, up_bias_grad = group_0[2:]
    own_part, *parts = back_to_tokens(
        n_tp, active, context, up_input_grad, projected_grad, down_weight, dense_weight, up_weight, parts_weight
    )

    (group_2,) = feed(slot_2, [slot_layout], *weights)

    slot_3, parts, group_2 = tie(slot_3, parts, group_2)
    got = [swap_tp(part, r + 1) for r, part in enumerate(parts)]
    (group_3,) = feed(slot_3, [slot_layout], *weights)

    groups = [group_0, group_1, group_2, group_3]
    normeds, upstreams, actives, up_grads = ([g[i] for g in groups] for i in range(4))
    up_part = outer_sum(line_place, normeds, up_grads)
    got, up_part, own_part, qkv_sum, dense_sum = tie(got, up_part, own_part, qkv_sum, dense_sum)
    other_up_part = swap_core(up_part)

    mixed, input_grad, sums = norm_back(tokens, upstream, gain, last_bias, own_part, *got)
    sums = sums + swap_tp(sums, 1)
    sums = sums + swap_tp(sums, 2)
    small = jnp.concatenate([sums.reshape(1, -1), qkv_bias_grad.reshape(1, -1), up_bias_grad], 1)
    small = small + swap_core(small)
    small = small + swap_line(small, 1)
    small = (small + swap_line(small, 2))[0]
    norm_gain_grad = small[:features]
    norm_bias_grad = small[features : 2 * features]
    out_bias_grad = small[2 * features : 3 * features]
    qkv_bias_grad = small[3 * features : 3 * features + 3 * heads_wide].reshape(3, heads_wide)
    up_bias_grad = small[3 * features + 3 * heads_wide :]

    down_part = outer_sum(line_place, actives, upstreams)
    other_down_part = swap_core(down_part)
    up_weight_grad = added(up_part, other_up_part)
    qkv_weight_grad = added(qkv_sum.reshape(3 * features, heads_wide), tile=features)
    qkv_weight_grad = qkv_weight_grad.reshape(3, features, heads_wide).transpose(1, 0, 2)
    dense_weight_grad = added(dense_sum)
    down_weight_grad = added(down_part, other_down_part)

    return (
        mixed,
        input_grad,
        norm_gain_grad,
        norm_bias_grad,
        qkv_weight_grad,
        qkv_bias_grad,
        dense_weight_grad,
        up_weight_grad,
        up_bias_grad,
        down_weight_grad,
        out_bias_grad,
    )


def allowed_block(segment_ids, positions, begin_row, block_rows):
    seg_rows = lax.dynamic_slice_in_dim(segment_ids, begin_row, block_rows)
    place_rows = lax.dynamic_slice_in_dim(positions, begin_row, block_rows)
    return (seg_rows[:, None] == segment_ids[None, :]) & (positions[None, :] <= place_rows[:, None])


def block_scores(query_block, keys_low, allowed):
    scores = (
        jnp.einsum("qhe,khe->hqk", query_block, keys_low, preferred_element_type=jnp.float32)
        * 0.125
    )
    return jnp.where(allowed[None], scores, masked_score)


def up_projection(gathered, up_weight, up_bias):
    up_input = jnp.dot(gathered, up_weight, preferred_element_type=jnp.float32) + up_bias.astype(
        jnp.float32
    )
    return (up_input, jax.nn.gelu(up_input, approximate=True).astype(jnp.bfloat16))


def row_product(left, right):
    return jnp.dot(left, right, preferred_element_type=jnp.float32)


def general_shards(
    tokens,
    upstream,
    segment_ids,
    positions,
    norm_gain,
    norm_bias,
    qkv_weight,
    qkv_bias,
    dense_weight,
    up_weight,
    up_bias,
    down_weight,
    out_bias,
):
    head_count = qkv_weight.shape[2] // HEAD_DIM
    inputs = tokens.astype(jnp.float32)
    normed_low = layer_norm(inputs, norm_gain, norm_bias).astype(jnp.bfloat16)
    gathered = lax.all_gather(normed_low, "tp", axis=0, tiled=True)
    group_rows = gathered.shape[0]
    block_rows = math.gcd(group_rows, 512)
    block_count = group_rows // block_rows
    projected = (
        jnp.einsum("td,dch->tch", gathered, qkv_weight, preferred_element_type=jnp.float32)
        + qkv_bias.astype(jnp.float32)[None]
    )
    head_shape = (group_rows, head_count, HEAD_DIM)
    cosine_table, sine_table = rotary_tables(positions, ROT)
    queries = rotate(projected[:, 0].reshape(head_shape), cosine_table, sine_table).astype(
        jnp.bfloat16
    )
    keys_low = rotate(projected[:, 1].reshape(head_shape), cosine_table, sine_table).astype(
        jnp.bfloat16
    )
    values_low = projected[:, 2].reshape(head_shape).astype(jnp.bfloat16)

    def forward_block(block_index):
        begin_row = block_index * block_rows
        query_block = lax.dynamic_slice_in_dim(queries, begin_row, block_rows, 0)
        scores = block_scores(
            query_block, keys_low, allowed_block(segment_ids, positions, begin_row, block_rows)
        )
        highest_score = jnp.max(scores, -1, keepdims=True)
        exponent = jnp.exp(scores - highest_score)
        totals = jnp.sum(exponent, -1, keepdims=True)
        soft_low = (exponent / totals).astype(jnp.bfloat16)
        context_block = jnp.einsum(
            "hqk,khe->qhe", soft_low, values_low, preferred_element_type=jnp.float32
        )
        return (context_block.astype(jnp.bfloat16), highest_score + jnp.log(totals))

    context_blocks, log_blocks = lax.map(forward_block, jnp.arange(block_count, dtype=jnp.int32))
    context_low = context_blocks.reshape(group_rows, head_count * HEAD_DIM)
    up_input, up_active_low = up_projection(gathered, up_weight, up_bias)
    summed = lax.psum_scatter(
        row_product(context_low, dense_weight) + row_product(up_active_low, down_weight),
        "tp",
        scatter_dimension=0,
        tiled=True,
    )
    mixed = (inputs + summed + out_bias).astype(jnp.bfloat16)
    upstream_all = lax.all_gather(upstream, "tp", axis=0, tiled=True)
    unit_column = jnp.ones((group_rows,), jnp.bfloat16)
    out_bias_grad = jnp.einsum(
        "t,td->d", unit_column, upstream_all, preferred_element_type=jnp.float32
    )
    dense_weight_grad = jnp.einsum(
        "te,td->ed", context_low, upstream_all, preferred_element_type=jnp.float32
    )
    down_weight_grad = jnp.einsum(
        "tf,td->fd", up_active_low, upstream_all, preferred_element_type=jnp.float32
    )
    context_grad = jnp.einsum(
        "td,ed->te", upstream_all, dense_weight, preferred_element_type=jnp.float32
    )
    context_grad_low = context_grad.astype(jnp.bfloat16).reshape(head_shape)
    active_grad = jnp.einsum(
        "td,fd->tf", upstream_all, down_weight, preferred_element_type=jnp.float32
    )
    _, gelu_back = jax.vjp(partial(jax.nn.gelu, approximate=True), up_input)
    up_input_grad = gelu_back(active_grad)[0].astype(jnp.bfloat16)
    up_bias_grad = jnp.einsum(
        "t,tf->f", unit_column, up_input_grad, preferred_element_type=jnp.float32
    )

    def backward_block(running, block_index):
        key_grad, value_grad = running
        begin_row = block_index * block_rows
        query_block = lax.dynamic_slice_in_dim(queries, begin_row, block_rows, 0)
        output_grad = lax.dynamic_slice_in_dim(context_grad_low, begin_row, block_rows, 0)
        log_totals = lax.dynamic_index_in_dim(log_blocks, block_index, 0, keepdims=False)
        scores = block_scores(
            query_block, keys_low, allowed_block(segment_ids, positions, begin_row, block_rows)
        )
        attn_soft = jnp.exp(scores - log_totals)
        value_grad = value_grad + jnp.einsum(
            "hqk,qhe->khe",
            attn_soft.astype(jnp.bfloat16),
            output_grad,
            preferred_element_type=jnp.float32,
        )
        prob_grad = jnp.einsum(
            "qhe,khe->hqk", output_grad, values_low, preferred_element_type=jnp.float32
        )
        row_dots = jnp.sum(attn_soft * prob_grad, -1, keepdims=True)
        score_grad = (attn_soft * (prob_grad - row_dots)).astype(jnp.bfloat16)
        query_grad = (
            jnp.einsum("hqk,khe->qhe", score_grad, keys_low, preferred_element_type=jnp.float32)
            * 0.125
        )
        key_grad = (
            key_grad
            + jnp.einsum(
                "hqk,qhe->khe", score_grad, query_block, preferred_element_type=jnp.float32
            )
            * 0.125
        )
        return ((key_grad, value_grad), query_grad)

    empty_grad = jnp.zeros(head_shape, jnp.float32)
    (key_grad, value_grad), query_blocks = lax.scan(
        backward_block, (empty_grad, empty_grad), jnp.arange(block_count, dtype=jnp.int32)
    )
    query_grad = query_blocks.reshape(head_shape)
    projected_grad = jnp.stack(
        [
            rotate(query_grad, cosine_table, -sine_table),
            rotate(key_grad, cosine_table, -sine_table),
            value_grad,
        ],
        axis=1,
    )
    projected_grad = projected_grad.reshape(group_rows, 3, head_count * HEAD_DIM).astype(
        jnp.bfloat16
    )
    qkv_bias_grad = jnp.einsum(
        "t,tch->ch", unit_column, projected_grad, preferred_element_type=jnp.float32
    )
    qkv_weight_grad = jnp.einsum(
        "td,tch->dch", gathered, projected_grad, preferred_element_type=jnp.float32
    )
    up_weight_grad = jnp.einsum(
        "td,tf->df", gathered, up_input_grad, preferred_element_type=jnp.float32
    )
    first = jnp.einsum(
        "tch,dch->td", projected_grad, qkv_weight, preferred_element_type=jnp.float32
    )
    normed_grad = lax.psum_scatter(
        first
        + jnp.einsum("tf,df->td", up_input_grad, up_weight, preferred_element_type=jnp.float32),
        "tp",
        scatter_dimension=0,
        tiled=True,
    )
    _, norm_back = jax.vjp(layer_norm, inputs, norm_gain, norm_bias)
    input_part, gain_part, shift_part = norm_back(normed_grad)
    input_grad = upstream.astype(jnp.float32) + input_part
    norm_gain_grad, norm_bias_grad = lax.psum((gain_part, shift_part), ("dp", "tp"))
    (
        qkv_weight_grad,
        qkv_bias_grad,
        dense_weight_grad,
        up_weight_grad,
        up_bias_grad,
        down_weight_grad,
        out_bias_grad,
    ) = lax.psum(
        (
            qkv_weight_grad,
            qkv_bias_grad,
            dense_weight_grad,
            up_weight_grad,
            up_bias_grad,
            down_weight_grad,
            out_bias_grad,
        ),
        "dp",
    )
    return (
        mixed,
        input_grad,
        norm_gain_grad,
        norm_bias_grad,
        qkv_weight_grad,
        qkv_bias_grad,
        dense_weight_grad,
        up_weight_grad,
        up_bias_grad,
        down_weight_grad,
        out_bias_grad,
    )


def solution(mesh):
    fits = mesh.shape["dp"] == 8 and mesh.shape["tp"] == 4
    return jax.shard_map(
        shards if fits else general_shards,
        mesh=mesh,
        in_specs=(
            P(("dp", "tp"), None),
            P(("dp", "tp"), None),
            P("dp"),
            P("dp"),
            P(),
            P(),
            P(None, None, "tp"),
            P(None, "tp"),
            P("tp", None),
            P(None, "tp"),
            P("tp"),
            P("tp", None),
            P(),
        ),
        out_specs=(
            P(("dp", "tp"), None),
            P(("dp", "tp"), None),
            P(),
            P(),
            P(None, None, "tp"),
            P(None, "tp"),
            P("tp", None),
            P(None, "tp"),
            P("tp"),
            P("tp", None),
            P(),
        ),
        check_vma=False,
    )
```

```python
from functools import partial
import math

import jax
import jax.numpy as jnp
from jax import lax
from jax.experimental import pallas as pl
from jax.experimental.pallas import tpu as pltpu
from jax.sharding import PartitionSpec as P

HEAD_DIM = 64
ROT = 32
norm_epsilon = 1e-05
masked_score = -1e30
low = jnp.bfloat16
wide = jnp.float32
VMEM = 56 * 2**20
HASTE = 0.02


def dot(left, right, left_dim, right_dim, kind=wide):
    return lax.dot_general(
        left, right, (((left_dim,), (right_dim,)), ((), ())), preferred_element_type=wide
    ).astype(kind)


def layer_norm(values, gain, shift):
    averaged = jnp.mean(values, -1, keepdims=True)
    centred = values - averaged
    spread = jnp.mean(centred * centred, -1, keepdims=True)
    return centred * lax.rsqrt(spread + norm_epsilon) * gain + shift


def rotary_tables(places, rot_dims):
    half_rot = rot_dims // 2
    frequency = jnp.power(10000.0, -2.0 * jnp.arange(half_rot).astype(wide) / rot_dims)
    phases = places.astype(wide)[:, None] * frequency[None, :]
    cosine_table = jnp.concatenate([jnp.cos(phases), jnp.cos(phases)], -1)[:, None, :]
    sine_table = jnp.concatenate([jnp.sin(phases), jnp.sin(phases)], -1)[:, None, :]
    return (cosine_table, sine_table)


def rotate(values, cosine_table, sine_table):
    rot_dims = cosine_table.shape[-1]
    half_rot = rot_dims // 2
    rotated_part = values[..., :rot_dims]
    turned = jnp.concatenate([-rotated_part[..., half_rot:], rotated_part[..., :half_rot]], -1)
    return jnp.concatenate(
        [rotated_part * cosine_table + turned * sine_table, values[..., rot_dims:]], -1
    )


def gelu_and_slope(v):
    inner = jnp.tanh(0.7978845608 * (v + 0.044715 * v * v * v))
    half = 0.5 * (1.0 + inner)
    slope = half + 0.5 * v * (1.0 - inner * inner) * 0.7978845608 * (1.0 + 0.134145 * v * v)
    return v * half, slope


def kernel_call(body, flops, out_shape, traffic=0, **kinds):
    return pl.pallas_call(
        body,
        out_shape=out_shape,
        compiler_params=pltpu.CompilerParams(vmem_limit_bytes=VMEM),
        cost_estimate=pl.CostEstimate(
            flops=int(flops * HASTE), bytes_accessed=traffic + int(flops * HASTE) // 512, transcendentals=0
        ),
        **kinds,
    )


def sds(shape, kind):
    return jax.ShapeDtypeStruct(shape, kind)


def whole_block(array):
    zeros = (0,) * array.ndim
    return pl.BlockSpec(array.shape, lambda *_: zeros, pipeline_mode=pl.Buffered(1))


def fixed_block(shape):
    zeros = (0,) * len(shape)
    return pl.BlockSpec(shape, lambda *_: zeros)


def assemble(target, pieces):
    at = 0
    for ref, first, size in pieces:
        target[at : at + size, :] = ref[first : first + size, :]
        at += size


def turned(values, cosine, sine_low, sine_high):
    return (
        values * cosine
        + pltpu.roll(values, 128 - ROT // 2, 1) * sine_low
        + pltpu.roll(values, ROT // 2, 1) * sine_high
    )


def row_means(inputs):
    centred = inputs - jnp.mean(inputs, -1, keepdims=True)
    spread = jnp.mean(centred * centred, -1, keepdims=True)
    scale = lax.rsqrt(spread + norm_epsilon)
    return centred * scale, scale


def norm_kernel(tokens, upstream, gain, shift, normed, both):
    unit, _ = row_means(tokens[...].astype(wide))
    rows = tokens.shape[0]
    normed[...] = (unit * gain[...] + shift[...]).astype(low)
    both[:rows, :] = normed[...]
    both[rows:, :] = upstream[...]


def norm_rows(tokens, upstream, gain, shift):
    rows, features = tokens.shape
    arrays = [tokens, upstream, gain, shift]
    return kernel_call(
        norm_kernel,
        rows * features * 512,
        [sds((rows, features), low), sds((2 * rows, features), low)],
        grid=(1,),
        in_specs=[whole_block(a) for a in arrays],
        out_specs=[fixed_block((rows, features)), fixed_block((2 * rows, features))],
    )(*arrays)


def norm_back_kernel(tokens, upstream, gain, out_bias, own, got_1, got_2, got_3, mixed, input_grad, sums):
    rows = tokens.shape[0]
    inputs, cotangent = tokens[...].astype(wide), upstream[...].astype(wide)

    def total(first):
        span = slice(first, first + rows)
        return (own[span, :] + got_1[span, :].astype(wide)) + (
            got_2[span, :].astype(wide) + got_3[span, :].astype(wide)
        )

    mixed[...] = (inputs + total(0) + out_bias[...]).astype(low)
    unit, scale = row_means(inputs)
    normed_grad = total(rows)
    e = normed_grad * gain[...]
    along = jnp.mean(e * unit, -1, keepdims=True)
    input_grad[...] = cotangent + (e - jnp.mean(e, -1, keepdims=True) - unit * along) * scale
    sums[0:1, :] = jnp.sum(normed_grad * unit, 0, keepdims=True)
    sums[1:2, :] = jnp.sum(normed_grad, 0, keepdims=True)
    sums[2:3, :] = jnp.sum(cotangent, 0, keepdims=True)


def norm_back(*arrays):
    rows, features = arrays[0].shape
    shapes = [(rows, features), (rows, features), (3, features)]
    return kernel_call(
        norm_back_kernel,
        rows * features * 1024,
        [sds(s, k) for s, k in zip(shapes, (low, wide, wide))],
        grid=(1,),
        in_specs=[whole_block(a) for a in arrays],
        out_specs=[fixed_block(s) for s in shapes],
    )(*arrays)


def project_kernel(count, *refs):
    weight, bias, cosine, sine_low, sine_high, rows_out, out = refs[count:]
    part = pl.program_id(0)

    @pl.when(part == 0)
    def _():
        assemble(rows_out, [(r, 0, r.shape[0]) for r in refs[:count]])

    projected = dot(rows_out[...], weight[0], 1, 0) + bias[0].astype(wide)

    @pl.when(part < 2)
    def _():
        scale = jnp.where(part == 0, 0.125, 1.0)
        for j in range(0, projected.shape[1], 128):
            rotated = turned(projected[:, j : j + 128], cosine[...], sine_low[...], sine_high[...])
            out[0, :, j : j + 128] = (rotated * scale).astype(low)

    @pl.when(part == 2)
    def _():
        out[0] = projected.astype(low)


def project(blocks, weight, bias, tables):
    tokens = sum(b.shape[0] for b in blocks)
    _, features, width = weight.shape
    table = whole_block(tables[0])
    return kernel_call(
        partial(project_kernel, len(blocks)),
        6 * tokens * features * width,
        [sds((tokens, features), low), sds((3, tokens, width), low)],
        grid=(3,),
        in_specs=[whole_block(a) for a in blocks]
        + [
            pl.BlockSpec((1, features, width), lambda c: (c, 0, 0)),
            pl.BlockSpec((1, 1, width), lambda c: (c, 0, 0)),
            table,
            table,
            table,
        ],
        out_specs=[fixed_block((tokens, features)), pl.BlockSpec((1, tokens, width), lambda c: (c, 0, 0))],
    )(*blocks, weight, bias, *tables)


def attention_kernel(count, *refs):
    (queries, keys, values, dense, seg_q, place_q, seg_k, place_k, cosine, sine_low, sine_high) = refs[count:-5]
    rows_out, context, out, bias_out, mask = refs[-5:]

    @pl.when(pl.program_id(0) == 0)
    def _():
        assemble(rows_out, [(r, 0, r.shape[0]) for r in refs[:count]])
        allowed = (seg_q[...] == seg_k[...]) & (place_k[...] <= place_q[...])
        mask[...] = jnp.where(allowed, 0.0, masked_score)

    q, k, v = queries[0], keys[0], values[0]
    g = dot(rows_out[...], dense[...], 1, 1, low)
    lane = lax.broadcasted_iota(jnp.int32, q.shape, 1) // HEAD_DIM
    found = []
    for head in range(128 // HEAD_DIM):
        mine = lane == head
        scores = dot(jnp.where(mine, q, jnp.zeros_like(q)), k, 1, 1) + mask[...]
        exponent = jnp.exp(scores - jnp.max(scores, -1, keepdims=True))
        soft = exponent * (1.0 / jnp.sum(exponent, -1, keepdims=True))
        soft_low = soft.astype(low)
        prob_grad = dot(jnp.where(mine, g, jnp.zeros_like(g)), v, 1, 1)
        row_dots = jnp.sum(soft * prob_grad, -1, keepdims=True)
        score_grad = (soft * (prob_grad - row_dots)).astype(low)
        found.append(
            (dot(soft_low, v, 1, 0), dot(score_grad, k, 1, 0), dot(score_grad, q, 0, 0), dot(soft_low, g, 0, 0))
        )
    parts = [jnp.where(lane == 0, a, b) for a, b in zip(*found)]
    context[...] = parts[0].astype(low)
    back = (cosine[...], -sine_low[...], -sine_high[...])
    grads = [turned(parts[1] * 0.125, *back), turned(parts[2], *back), parts[3]]
    for c, value in enumerate(grads):
        rounded = value.astype(low)
        out[c] = rounded
        bias_out[c] = jnp.sum(rounded.astype(wide), 0, keepdims=True)


def attention(blocks, qkv, dense_weight, seg, place, tables):
    _, tokens, width = qkv.shape
    features = dense_weight.shape[1]
    column, row = (lambda a: a.reshape(tokens, 1)), (lambda a: a.reshape(1, tokens))
    extras = [column(seg), column(place), row(seg), row(place), *tables]
    part = lambda c: pl.BlockSpec((1, tokens, 128), lambda j: (c, 0, j))
    return kernel_call(
        partial(attention_kernel, len(blocks)),
        20 * tokens * tokens * width,
        [
            sds((tokens, features), low),
            sds((tokens, width), low),
            sds((3, tokens, width), low),
            sds((3, 1, width), wide),
        ],
        grid=(width // 128,),
        in_specs=[whole_block(b) for b in blocks]
        + [part(0), part(1), part(2), pl.BlockSpec((128, features), lambda j: (j, 0))]
        + [whole_block(e) for e in extras],
        out_specs=[
            fixed_block((tokens, features)),
            pl.BlockSpec((tokens, 128), lambda j: (0, j)),
            pl.BlockSpec((3, tokens, 128), lambda j: (0, 0, j)),
            pl.BlockSpec((3, 1, 128), lambda j: (0, 0, j)),
        ],
        scratch_shapes=[pltpu.VMEM((tokens, tokens), wide)],
    )(*blocks, qkv, qkv, qkv, dense_weight, *extras)


def outer_pair_kernel(n_first, left, right, context, upstream, out):
    step = pl.program_id(0)

    @pl.when(step < n_first)
    def _():
        out[...] = dot(left[...], right[0], 0, 0, low)

    @pl.when(step >= n_first)
    def _():
        found = dot(context[...], upstream[...], 0, 0, low)
        width = context.shape[1]
        for i in range(found.shape[1] // width):
            out[i * width : (i + 1) * width, :] = found[:, i * width : (i + 1) * width]


def outer_pair(left, right, context, upstream, tile=1024):
    count, tokens, width = right.shape
    features = left.shape[1]
    each = features // tile
    n_first = count * each
    return kernel_call(
        partial(outer_pair_kernel, n_first),
        2 * (count + 1) * tokens * features * width,
        sds(((count + 1) * features, width), low),
        grid=(n_first + each,),
        in_specs=[
            pl.BlockSpec((tokens, tile), lambda s: (0, jnp.where(s < n_first, s % each, each - 1))),
            pl.BlockSpec((1, tokens, width), lambda s: (jnp.minimum(s // each, count - 1), 0, 0)),
            whole_block(context),
            pl.BlockSpec((tokens, tile), lambda s: (0, jnp.maximum(s - n_first, 0))),
        ],
        out_specs=pl.BlockSpec((tile, width), lambda s: (s, 0)),
    )(left, right, context, upstream)


def widen_pair_kernel(n_first, given, first, second):
    step = pl.program_id(0)

    @pl.when(step < n_first)
    def _():
        first[...] = given[...].astype(wide)

    @pl.when(step >= n_first)
    def _():
        width = given.shape[1]
        for i in range(given.shape[0] // width):
            second[:, i * width : (i + 1) * width] = given[i * width : (i + 1) * width, :].astype(wide)


def widen_pair(given, features, tile=1024):
    rows, width = given.shape
    each = features // tile
    n_first = rows // tile - each
    return kernel_call(
        partial(widen_pair_kernel, n_first),
        rows * width * 256,
        [sds((rows - features, width), wide), sds((width, features), wide)],
        6 * rows * width,
        grid=(n_first + each,),
        in_specs=[pl.BlockSpec((tile, width), lambda s: (s, 0))],
        out_specs=[
            pl.BlockSpec((tile, width), lambda s: (jnp.minimum(s, n_first - 1), 0)),
            pl.BlockSpec((width, tile), lambda s: (0, jnp.maximum(s - n_first, 0))),
        ],
    )(given)


def feed_kernel(layouts, n_arrays, *refs):
    arrays, refs = refs[:n_arrays], refs[n_arrays:]
    up_weight, down_weight, up_bias = refs[:3]
    outs = refs[3:]
    pick = lambda layout: [(arrays[i], first, size) for i, first, size in layout]

    @pl.when(pl.program_id(0) == 0)
    def _():
        for (normed_layout, upstream_layout), (normed_out, upstream_out, *_) in zip(layouts, fives(outs)):
            assemble(normed_out, pick(normed_layout))
            assemble(upstream_out, pick(upstream_layout))

    bias = up_bias[...].astype(wide)
    for normed_out, upstream_out, active_out, grad_out, sum_out in fives(outs):
        active, slope = gelu_and_slope(dot(normed_out[...], up_weight[...], 1, 0) + bias)
        active_out[...] = active.astype(low)
        rounded = (dot(upstream_out[...], down_weight[...], 1, 1) * slope).astype(low)
        grad_out[...] = rounded
        sum_out[...] = jnp.sum(rounded.astype(wide), 0, keepdims=True)


def fives(outs):
    return [outs[i : i + 5] for i in range(0, len(outs), 5)]


def feed(arrays, layouts, up_weight, down_weight, up_bias, tile=512):
    features, hidden = up_weight.shape
    tokens = sum(size for _, _, size in layouts[0][0])
    rows_spec = fixed_block((tokens, features))
    tile_spec = pl.BlockSpec((tokens, tile), lambda j: (0, j))
    sum_spec = pl.BlockSpec((1, tile), lambda j: (0, j))
    shapes = [sds((tokens, features), low)] * 2 + [sds((tokens, hidden), low)] * 2 + [sds((1, hidden), wide)]
    found = kernel_call(
        partial(feed_kernel, layouts, len(arrays)),
        4 * len(layouts) * tokens * features * hidden,
        shapes * len(layouts),
        grid=(hidden // tile,),
        in_specs=[whole_block(a) for a in arrays]
        + [
            pl.BlockSpec((features, tile), lambda j: (0, j)),
            pl.BlockSpec((tile, features), lambda j: (j, 0)),
            pl.BlockSpec((1, tile), lambda j: (0, j)),
        ],
        out_specs=[rows_spec, rows_spec, tile_spec, tile_spec, sum_spec] * len(layouts),
    )(*arrays, up_weight, down_weight, up_bias)
    return fives(found)


def back_kernel(n_tp, active, context, up_grad, part_grad, down, dense, up, part_weight, own, *sent):
    rows = active.shape[0] // n_tp
    mixed = dot(active[...], down[...], 1, 0) + dot(context[...], dense[...], 1, 0)
    normed_grad = dot(up_grad[...], up[...], 1, 1)
    for c in range(3):
        normed_grad = normed_grad + dot(part_grad[c], part_weight[c], 1, 1)
    for i, value in enumerate((mixed, normed_grad)):
        span = slice(i * rows, (i + 1) * rows)
        own[span, :] = value[:rows]
        for r in range(1, n_tp):
            sent[r - 1][span, :] = value[r * rows : (r + 1) * rows].astype(low)


def back_to_tokens(n_tp, active, context, up_grad, part_grad, down, dense, up, part_weight, tile=512):
    tokens, hidden = active.shape
    features, width = down.shape[1], context.shape[1]
    rows = 2 * tokens // n_tp
    column = pl.BlockSpec((rows, tile), lambda j: (0, j))
    return kernel_call(
        partial(back_kernel, n_tp),
        4 * tokens * features * (hidden + 2 * width),
        [sds((rows, features), wide)] + [sds((rows, features), low)] * (n_tp - 1),
        grid=(features // tile,),
        in_specs=[whole_block(a) for a in (active, context, up_grad, part_grad)]
        + [
            pl.BlockSpec((hidden, tile), lambda j: (0, j)),
            pl.BlockSpec((width, tile), lambda j: (0, j)),
            pl.BlockSpec((tile, hidden), lambda j: (j, 0)),
            pl.BlockSpec((3, tile, width), lambda j: (0, j, 0)),
        ],
        out_specs=[column] * n_tp,
    )(active, context, up_grad, part_grad, down, dense, up, part_weight)


def outer_kernel(count, place, *refs):
    out = refs[2 * count]
    for here in range(count):

        @pl.when(place[0] == here)
        def _():
            total = None
            for there in range(count):
                i = here ^ there
                term = dot(refs[i][...], refs[count + i][...], 0, 0)
                total = term if total is None else total + term
            out[...] = total.astype(out.dtype)


def outer_sum(place, lefts, rights, tile_m=512, tile_n=1024):
    count, (tokens, m), n = len(lefts), lefts[0].shape, rights[0].shape[1]
    return kernel_call(
        partial(outer_kernel, count),
        2 * count * tokens * m * n,
        sds((m, n), low),
        grid_spec=pltpu.PrefetchScalarGridSpec(
            num_scalar_prefetch=1,
            grid=(n // tile_n, m // tile_m),
            in_specs=[pl.BlockSpec((tokens, tile_m), lambda j, i, _: (0, i))] * count
            + [pl.BlockSpec((tokens, tile_n), lambda j, i, _: (0, j))] * count,
            out_specs=pl.BlockSpec((tile_m, tile_n), lambda j, i, _: (i, j)),
        ),
    )(place.reshape(1).astype(jnp.int32), *lefts, *rights)


def add_kernel(*refs):
    total = refs[0][...].astype(wide)
    for ref in refs[1:-1]:
        total = total + ref[...].astype(wide)
    refs[-1][...] = total


def added(*terms, tile=512):
    m, n = terms[0].shape
    spec = pl.BlockSpec((tile, n), lambda i: (i, 0))
    return kernel_call(
        add_kernel, m * n * 256, sds((m, n), wide), 8 * m * n, grid=(m // tile,), in_specs=[spec] * len(terms), out_specs=spec
    )(*terms)


def tie(*arrays):
    return lax.optimization_barrier(arrays)


def shards(
    tokens,
    upstream,
    segment_ids,
    positions,
    norm_gain,
    norm_bias,
    qkv_weight,
    qkv_bias,
    dense_weight,
    up_weight,
    up_bias,
    down_weight,
    out_bias,
):
    n_tp, n_line = 4, 4
    dp_place, tp_place = lax.axis_index("dp"), lax.axis_index("tp")
    line_place = dp_place // 2
    rows, features = tokens.shape
    group_rows = rows * n_tp
    heads_wide = qkv_weight.shape[2]
    hidden = up_weight.shape[1]

    def swap_tp(array, flip):
        return lax.ppermute(array, "tp", [(i, i ^ flip) for i in range(n_tp)])

    def swap_core(array):
        return lax.ppermute(array, "dp", [(i, i ^ 1) for i in range(2 * n_line)])

    def swap_line(array, flip):
        return lax.ppermute(array, "dp", [(i, i ^ (2 * flip)) for i in range(2 * n_line)])

    def hop(array, pairs):
        return lax.ppermute(array, "dp", [(2 * s + c, 2 * d + c) for s, d in pairs for c in (0, 1)])

    def to_neighbours(block):
        return swap_tp(block, 1), swap_tp(block, 2)

    def to_diagonal(block_1, block_2):
        size = block_1.shape[0] // 2
        return swap_tp(block_1[:size], 2), swap_tp(block_2[size:], 1)

    def from_others(array):
        return [swap_tp(array, r) for r in range(1, n_tp)]

    upstream_r1, upstream_r2 = to_neighbours(upstream)
    gain, shift, last_bias = (a.reshape(1, features) for a in (norm_gain, norm_bias, out_bias))
    normed, both = norm_rows(tokens, upstream, gain, shift)
    normed_blocks = [normed, *from_others(normed)]
    above_1, below_1 = hop(both, [(0, 1), (1, 2), (2, 3)]), hop(both, [(1, 0), (2, 1), (3, 2)])

    by_owner = jnp.stack([segment_ids.reshape(n_tp, rows), positions.reshape(n_tp, rows)])
    owner = tp_place ^ jnp.arange(n_tp)
    pick = (owner[:, None] == jnp.arange(n_tp)[None, :]).astype(jnp.int32)
    arranged = jnp.sum(pick[None, :, :, None] * by_owner[:, None, :, :], 2).reshape(2, group_rows)
    seg, place = arranged[0], arranged[1]
    cosine_table, sine_table = rotary_tables(place, ROT)
    cosine, sine = cosine_table[:, 0, :], sine_table[:, 0, :]
    still = jnp.zeros((group_rows, HEAD_DIM - ROT), wide)
    quiet = jnp.zeros((group_rows, ROT // 2), wide)
    tables = [
        jnp.concatenate([cosine, still + 1.0], 1),
        jnp.concatenate([-sine[:, : ROT // 2], quiet, still], 1),
        jnp.concatenate([quiet, sine[:, : ROT // 2], still], 1),
    ]
    tables = [jnp.concatenate([t] * (128 // HEAD_DIM), 1) for t in tables]
    parts_weight = qkv_weight.transpose(1, 0, 2)
    parts_bias = qkv_bias.reshape(3, 1, heads_wide)

    upstream_r1, upstream_r2, tables, seg, place = tie(upstream_r1, upstream_r2, tables, seg, place)
    upstream_r3 = to_diagonal(upstream_r1, upstream_r2)
    normed_blocks, tables, above_1, below_1 = tie(normed_blocks, tables, above_1, below_1)
    above_2, below_2 = hop(above_1, [(1, 2), (2, 3)]), hop(below_1, [(1, 0), (2, 1)])
    group_normed, qkv = project(normed_blocks, parts_weight, parts_bias, tables)

    slot_1 = jnp.where(line_place % 2 == 1, above_1, below_1)
    group_normed, qkv, upstream_r3, slot_1 = tie(group_normed, qkv, upstream_r3, slot_1)
    slot_1_r1, slot_1_r2 = to_neighbours(slot_1)
    upstream_blocks = [upstream, upstream_r1, upstream_r2, *upstream_r3]
    group_upstream, context, projected_grad, qkv_bias_grad = attention(
        upstream_blocks, qkv, dense_weight, seg, place, tables
    )

    slot_1_r1, slot_1_r2, above_2, below_2, group_upstream, context, projected_grad = tie(
        slot_1_r1, slot_1_r2, above_2, below_2, group_upstream, context, projected_grad
    )
    above_3, below_3 = hop(above_2, [(2, 3)]), hop(below_2, [(1, 0)])
    slot_1_r3 = to_diagonal(slot_1_r1, slot_1_r2)
    slot_2 = jnp.where(line_place >= 2, above_2, below_2)
    pair_part = outer_pair(group_normed, projected_grad, context, group_upstream)

    slot_layout = (
        [(0, 0, rows), (1, 0, rows), (2, 0, rows), (3, 0, rows)],
        [(0, rows, rows), (1, rows, rows), (2, rows, rows), (4, 0, rows)],
    )
    own_layout = ([(0, 0, group_rows)], [(1, 0, group_rows)])
    weights = (up_weight, down_weight, up_bias.reshape(1, hidden))
    group_normed, group_upstream, context, projected_grad, pair_part, above_3, below_3, slot_1_r3 = tie(
        group_normed, group_upstream, context, projected_grad, pair_part, above_3, below_3, slot_1_r3
    )
    slot_2_r1, slot_2_r2 = to_neighbours(slot_2)
    pair_share = lax.psum_scatter(pair_part, "dp", scatter_dimension=0, tiled=True)
    (group_0,) = feed([group_normed, group_upstream], [own_layout], *weights)
    (group_1,) = feed([slot_1, slot_1_r1, slot_1_r2, *slot_1_r3], [slot_layout], *weights)

    slot_2_r1, slot_2_r2, group_0, group_1 = tie(slot_2_r1, slot_2_r2, group_0, group_1)
    slot_3 = jnp.where(
        line_place == 0, below_3, jnp.where(line_place == 1, below_1, jnp.where(line_place == 2, above_1, above_3))
    )
    slot_2_r3 = to_diagonal(slot_2_r1, slot_2_r2)
    slot_3_r1, slot_3_r2 = to_neighbours(slot_3)
    active, up_input_grad, up_bias_grad = group_0[2:]
    own_part, *parts = back_to_tokens(
        n_tp, active, context, up_input_grad, projected_grad, down_weight, dense_weight, up_weight, parts_weight
    )

    slot_2_r3, own_part, parts, slot_3_r1, slot_3_r2 = tie(slot_2_r3, own_part, parts, slot_3_r1, slot_3_r2)
    slot_3_r3 = to_diagonal(slot_3_r1, slot_3_r2)
    (group_2,) = feed([slot_2, slot_2_r1, slot_2_r2, *slot_2_r3], [slot_layout], *weights)

    slot_3_r3, parts, group_2 = tie(slot_3_r3, parts, group_2)
    got = [swap_tp(part, r + 1) for r, part in enumerate(parts)]
    (group_3,) = feed([slot_3, slot_3_r1, slot_3_r2, *slot_3_r3], [slot_layout], *weights)

    group_3, pair_share = tie(group_3, pair_share)
    pair_sum = lax.all_gather(pair_share, "dp", axis=0, tiled=True)

    groups = [group_0, group_1, group_2, group_3]
    normeds, upstreams, actives, up_grads = ([g[i] for g in groups] for i in range(4))
    up_part = outer_sum(line_place, normeds, up_grads)
    up_part, actives, upstreams = tie(up_part, list(actives), list(upstreams))
    other_up_part = swap_core(up_part)
    down_part = outer_sum(line_place, actives, upstreams)
    got, own_part, down_part = tie(got, own_part, down_part)
    other_down_part = swap_core(down_part)
    mixed, input_grad, sums = norm_back(tokens, upstream, gain, last_bias, own_part, *got)
    turn = swap_tp(sums, 1)
    up_weight_grad = added(up_part, other_up_part)
    turn, up_weight_grad = tie(turn, up_weight_grad)
    sums = sums + turn
    turn = swap_tp(sums, 2)
    down_weight_grad = added(down_part, other_down_part)
    turn, down_weight_grad, pair_sum = tie(turn, down_weight_grad, pair_sum)
    sums = sums + turn
    small = jnp.concatenate([sums.reshape(1, -1), qkv_bias_grad.reshape(1, -1), up_bias_grad], 1)
    turn = swap_core(small)
    qkv_weight_grad, dense_weight_grad = widen_pair(pair_sum, features)
    qkv_weight_grad = qkv_weight_grad.reshape(3, features, heads_wide).transpose(1, 0, 2)
    turn, qkv_weight_grad = tie(turn, qkv_weight_grad)
    small = small + turn
    small = small + swap_line(small, 1)
    small = (small + swap_line(small, 2))[0]
    norm_gain_grad = small[:features]
    norm_bias_grad = small[features : 2 * features]
    out_bias_grad = small[2 * features : 3 * features]
    qkv_bias_grad = small[3 * features : 3 * features + 3 * heads_wide].reshape(3, heads_wide)
    up_bias_grad = small[3 * features + 3 * heads_wide :]

    return (
        mixed,
        input_grad,
        norm_gain_grad,
        norm_bias_grad,
        qkv_weight_grad,
        qkv_bias_grad,
        dense_weight_grad,
        up_weight_grad,
        up_bias_grad,
        down_weight_grad,
        out_bias_grad,
    )


def allowed_block(segment_ids, positions, begin_row, block_rows):
    seg_rows = lax.dynamic_slice_in_dim(segment_ids, begin_row, block_rows)
    place_rows = lax.dynamic_slice_in_dim(positions, begin_row, block_rows)
    return (seg_rows[:, None] == segment_ids[None, :]) & (positions[None, :] <= place_rows[:, None])


def block_scores(query_block, keys_low, allowed):
    scores = (
        jnp.einsum("qhe,khe->hqk", query_block, keys_low, preferred_element_type=jnp.float32)
        * 0.125
    )
    return jnp.where(allowed[None], scores, masked_score)


def up_projection(gathered, up_weight, up_bias):
    up_input = jnp.dot(gathered, up_weight, preferred_element_type=jnp.float32) + up_bias.astype(
        jnp.float32
    )
    return (up_input, jax.nn.gelu(up_input, approximate=True).astype(jnp.bfloat16))


def row_product(left, right):
    return jnp.dot(left, right, preferred_element_type=jnp.float32)


def general_shards(
    tokens,
    upstream,
    segment_ids,
    positions,
    norm_gain,
    norm_bias,
    qkv_weight,
    qkv_bias,
    dense_weight,
    up_weight,
    up_bias,
    down_weight,
    out_bias,
):
    head_count = qkv_weight.shape[2] // HEAD_DIM
    inputs = tokens.astype(jnp.float32)
    normed_low = layer_norm(inputs, norm_gain, norm_bias).astype(jnp.bfloat16)
    gathered = lax.all_gather(normed_low, "tp", axis=0, tiled=True)
    group_rows = gathered.shape[0]
    block_rows = math.gcd(group_rows, 512)
    block_count = group_rows // block_rows
    projected = (
        jnp.einsum("td,dch->tch", gathered, qkv_weight, preferred_element_type=jnp.float32)
        + qkv_bias.astype(jnp.float32)[None]
    )
    head_shape = (group_rows, head_count, HEAD_DIM)
    cosine_table, sine_table = rotary_tables(positions, ROT)
    queries = rotate(projected[:, 0].reshape(head_shape), cosine_table, sine_table).astype(
        jnp.bfloat16
    )
    keys_low = rotate(projected[:, 1].reshape(head_shape), cosine_table, sine_table).astype(
        jnp.bfloat16
    )
    values_low = projected[:, 2].reshape(head_shape).astype(jnp.bfloat16)

    def forward_block(block_index):
        begin_row = block_index * block_rows
        query_block = lax.dynamic_slice_in_dim(queries, begin_row, block_rows, 0)
        scores = block_scores(
            query_block, keys_low, allowed_block(segment_ids, positions, begin_row, block_rows)
        )
        highest_score = jnp.max(scores, -1, keepdims=True)
        exponent = jnp.exp(scores - highest_score)
        totals = jnp.sum(exponent, -1, keepdims=True)
        soft_low = (exponent / totals).astype(jnp.bfloat16)
        context_block = jnp.einsum(
            "hqk,khe->qhe", soft_low, values_low, preferred_element_type=jnp.float32
        )
        return (context_block.astype(jnp.bfloat16), highest_score + jnp.log(totals))

    context_blocks, log_blocks = lax.map(forward_block, jnp.arange(block_count, dtype=jnp.int32))
    context_low = context_blocks.reshape(group_rows, head_count * HEAD_DIM)
    up_input, up_active_low = up_projection(gathered, up_weight, up_bias)
    summed = lax.psum_scatter(
        row_product(context_low, dense_weight) + row_product(up_active_low, down_weight),
        "tp",
        scatter_dimension=0,
        tiled=True,
    )
    mixed = (inputs + summed + out_bias).astype(jnp.bfloat16)
    upstream_all = lax.all_gather(upstream, "tp", axis=0, tiled=True)
    unit_column = jnp.ones((group_rows,), jnp.bfloat16)
    out_bias_grad = jnp.einsum(
        "t,td->d", unit_column, upstream_all, preferred_element_type=jnp.float32
    )
    dense_weight_grad = jnp.einsum(
        "te,td->ed", context_low, upstream_all, preferred_element_type=jnp.float32
    )
    down_weight_grad = jnp.einsum(
        "tf,td->fd", up_active_low, upstream_all, preferred_element_type=jnp.float32
    )
    context_grad = jnp.einsum(
        "td,ed->te", upstream_all, dense_weight, preferred_element_type=jnp.float32
    )
    context_grad_low = context_grad.astype(jnp.bfloat16).reshape(head_shape)
    active_grad = jnp.einsum(
        "td,fd->tf", upstream_all, down_weight, preferred_element_type=jnp.float32
    )
    _, gelu_back = jax.vjp(partial(jax.nn.gelu, approximate=True), up_input)
    up_input_grad = gelu_back(active_grad)[0].astype(jnp.bfloat16)
    up_bias_grad = jnp.einsum(
        "t,tf->f", unit_column, up_input_grad, preferred_element_type=jnp.float32
    )

    def backward_block(running, block_index):
        key_grad, value_grad = running
        begin_row = block_index * block_rows
        query_block = lax.dynamic_slice_in_dim(queries, begin_row, block_rows, 0)
        output_grad = lax.dynamic_slice_in_dim(context_grad_low, begin_row, block_rows, 0)
        log_totals = lax.dynamic_index_in_dim(log_blocks, block_index, 0, keepdims=False)
        scores = block_scores(
            query_block, keys_low, allowed_block(segment_ids, positions, begin_row, block_rows)
        )
        attn_soft = jnp.exp(scores - log_totals)
        value_grad = value_grad + jnp.einsum(
            "hqk,qhe->khe",
            attn_soft.astype(jnp.bfloat16),
            output_grad,
            preferred_element_type=jnp.float32,
        )
        prob_grad = jnp.einsum(
            "qhe,khe->hqk", output_grad, values_low, preferred_element_type=jnp.float32
        )
        row_dots = jnp.sum(attn_soft * prob_grad, -1, keepdims=True)
        score_grad = (attn_soft * (prob_grad - row_dots)).astype(jnp.bfloat16)
        query_grad = (
            jnp.einsum("hqk,khe->qhe", score_grad, keys_low, preferred_element_type=jnp.float32)
            * 0.125
        )
        key_grad = (
            key_grad
            + jnp.einsum(
                "hqk,qhe->khe", score_grad, query_block, preferred_element_type=jnp.float32
            )
            * 0.125
        )
        return ((key_grad, value_grad), query_grad)

    empty_grad = jnp.zeros(head_shape, jnp.float32)
    (key_grad, value_grad), query_blocks = lax.scan(
        backward_block, (empty_grad, empty_grad), jnp.arange(block_count, dtype=jnp.int32)
    )
    query_grad = query_blocks.reshape(head_shape)
    projected_grad = jnp.stack(
        [
            rotate(query_grad, cosine_table, -sine_table),
            rotate(key_grad, cosine_table, -sine_table),
            value_grad,
        ],
        axis=1,
    )
    projected_grad = projected_grad.reshape(group_rows, 3, head_count * HEAD_DIM).astype(
        jnp.bfloat16
    )
    qkv_bias_grad = jnp.einsum(
        "t,tch->ch", unit_column, projected_grad, preferred_element_type=jnp.float32
    )
    qkv_weight_grad = jnp.einsum(
        "td,tch->dch", gathered, projected_grad, preferred_element_type=jnp.float32
    )
    up_weight_grad = jnp.einsum(
        "td,tf->df", gathered, up_input_grad, preferred_element_type=jnp.float32
    )
    first = jnp.einsum(
        "tch,dch->td", projected_grad, qkv_weight, preferred_element_type=jnp.float32
    )
    normed_grad = lax.psum_scatter(
        first
        + jnp.einsum("tf,df->td", up_input_grad, up_weight, preferred_element_type=jnp.float32),
        "tp",
        scatter_dimension=0,
        tiled=True,
    )
    _, norm_back = jax.vjp(layer_norm, inputs, norm_gain, norm_bias)
    input_part, gain_part, shift_part = norm_back(normed_grad)
    input_grad = upstream.astype(jnp.float32) + input_part
    norm_gain_grad, norm_bias_grad = lax.psum((gain_part, shift_part), ("dp", "tp"))
    (
        qkv_weight_grad,
        qkv_bias_grad,
        dense_weight_grad,
        up_weight_grad,
        up_bias_grad,
        down_weight_grad,
        out_bias_grad,
    ) = lax.psum(
        (
            qkv_weight_grad,
            qkv_bias_grad,
            dense_weight_grad,
            up_weight_grad,
            up_bias_grad,
            down_weight_grad,
            out_bias_grad,
        ),
        "dp",
    )
    return (
        mixed,
        input_grad,
        norm_gain_grad,
        norm_bias_grad,
        qkv_weight_grad,
        qkv_bias_grad,
        dense_weight_grad,
        up_weight_grad,
        up_bias_grad,
        down_weight_grad,
        out_bias_grad,
    )


def solution(mesh):
    fits = mesh.shape["dp"] == 8 and mesh.shape["tp"] == 4
    return jax.shard_map(
        shards if fits else general_shards,
        mesh=mesh,
        in_specs=(
            P(("dp", "tp"), None),
            P(("dp", "tp"), None),
            P("dp"),
            P("dp"),
            P(),
            P(),
            P(None, None, "tp"),
            P(None, "tp"),
            P("tp", None),
            P(None, "tp"),
            P("tp"),
            P("tp", None),
            P(),
        ),
        out_specs=(
            P(("dp", "tp"), None),
            P(("dp", "tp"), None),
            P(),
            P(),
            P(None, None, "tp"),
            P(None, "tp"),
            P("tp", None),
            P(None, "tp"),
            P("tp"),
            P("tp", None),
            P(),
        ),
        check_vma=False,
    )
```

```python
from functools import partial
import math

import jax
import jax.numpy as jnp
from jax import lax
from jax.experimental import pallas as pl
from jax.experimental.pallas import tpu as pltpu
from jax.sharding import PartitionSpec as P

HEAD_DIM = 64
ROT = 32
norm_epsilon = 1e-05
masked_score = -1e30
low = jnp.bfloat16
wide = jnp.float32
VMEM = 56 * 2**20
HASTE = 0.02
LANES = 256


def dot(left, right, left_dim, right_dim, kind=wide):
    return lax.dot_general(
        left, right, (((left_dim,), (right_dim,)), ((), ())), preferred_element_type=wide
    ).astype(kind)


def layer_norm(values, gain, shift):
    averaged = jnp.mean(values, -1, keepdims=True)
    centred = values - averaged
    spread = jnp.mean(centred * centred, -1, keepdims=True)
    return centred * lax.rsqrt(spread + norm_epsilon) * gain + shift


def rotary_tables(places, rot_dims):
    half_rot = rot_dims // 2
    frequency = jnp.power(10000.0, -2.0 * jnp.arange(half_rot).astype(wide) / rot_dims)
    phases = places.astype(wide)[:, None] * frequency[None, :]
    cosine_table = jnp.concatenate([jnp.cos(phases), jnp.cos(phases)], -1)[:, None, :]
    sine_table = jnp.concatenate([jnp.sin(phases), jnp.sin(phases)], -1)[:, None, :]
    return (cosine_table, sine_table)


def rotate(values, cosine_table, sine_table):
    rot_dims = cosine_table.shape[-1]
    half_rot = rot_dims // 2
    rotated_part = values[..., :rot_dims]
    turned = jnp.concatenate([-rotated_part[..., half_rot:], rotated_part[..., :half_rot]], -1)
    return jnp.concatenate(
        [rotated_part * cosine_table + turned * sine_table, values[..., rot_dims:]], -1
    )


def gelu_and_slope(v):
    square = v * v
    inner = jnp.tanh(v * (0.7978845608 + 0.035677408137 * square))
    half = 0.5 + 0.5 * inner
    slope = half + (v - v * (inner * inner)) * (0.3989422804 + 0.0535161122 * square)
    return v * half, slope


def kernel_call(body, flops, out_shape, traffic=0, **kinds):
    return pl.pallas_call(
        body,
        out_shape=out_shape,
        compiler_params=pltpu.CompilerParams(vmem_limit_bytes=VMEM),
        cost_estimate=pl.CostEstimate(
            flops=int(flops * HASTE), bytes_accessed=traffic + int(flops * HASTE) // 512, transcendentals=0
        ),
        **kinds,
    )


def sds(shape, kind):
    return jax.ShapeDtypeStruct(shape, kind)


def whole_block(array):
    zeros = (0,) * array.ndim
    return pl.BlockSpec(array.shape, lambda *_: zeros, pipeline_mode=pl.Buffered(1))


def fixed_block(shape):
    zeros = (0,) * len(shape)
    return pl.BlockSpec(shape, lambda *_: zeros)


def assemble(target, pieces):
    at = 0
    for ref, first, size in pieces:
        target[at : at + size, :] = ref[first : first + size, :]
        at += size


def turned(values, cosine, sine_low, sine_high):
    return (
        values * cosine
        + pltpu.roll(values, 128 - ROT // 2, 1) * sine_low
        + pltpu.roll(values, ROT // 2, 1) * sine_high
    )


def row_means(inputs):
    centred = inputs - jnp.mean(inputs, -1, keepdims=True)
    spread = jnp.mean(centred * centred, -1, keepdims=True)
    scale = lax.rsqrt(spread + norm_epsilon)
    return centred * scale, scale


def norm_kernel(tokens, upstream, gain, shift, normed, both):
    unit, _ = row_means(tokens[...].astype(wide))
    rows = tokens.shape[0]
    normed[...] = (unit * gain[...] + shift[...]).astype(low)
    both[:rows, :] = normed[...]
    both[rows:, :] = upstream[...]


def norm_rows(tokens, upstream, gain, shift):
    rows, features = tokens.shape
    arrays = [tokens, upstream, gain, shift]
    return kernel_call(
        norm_kernel,
        rows * features * 512,
        [sds((rows, features), low), sds((2 * rows, features), low)],
        grid=(1,),
        in_specs=[whole_block(a) for a in arrays],
        out_specs=[fixed_block((rows, features)), fixed_block((2 * rows, features))],
    )(*arrays)


def norm_back_kernel(tokens, upstream, gain, out_bias, own, got_1, got_2, got_3, mixed, input_grad, sums):
    rows = tokens.shape[0]
    inputs, cotangent = tokens[...].astype(wide), upstream[...].astype(wide)

    def total(first):
        span = slice(first, first + rows)
        return (own[span, :] + got_1[span, :].astype(wide)) + (
            got_2[span, :].astype(wide) + got_3[span, :].astype(wide)
        )

    mixed[...] = (inputs + total(0) + out_bias[...]).astype(low)
    unit, scale = row_means(inputs)
    normed_grad = total(rows)
    e = normed_grad * gain[...]
    along = jnp.mean(e * unit, -1, keepdims=True)
    input_grad[...] = cotangent + (e - jnp.mean(e, -1, keepdims=True) - unit * along) * scale
    sums[0:1, :] = jnp.sum(normed_grad * unit, 0, keepdims=True)
    sums[1:2, :] = jnp.sum(normed_grad, 0, keepdims=True)
    sums[2:3, :] = jnp.sum(cotangent, 0, keepdims=True)


def norm_back(*arrays):
    rows, features = arrays[0].shape
    shapes = [(rows, features), (rows, features), (3, features)]
    return kernel_call(
        norm_back_kernel,
        rows * features * 1024,
        [sds(s, k) for s, k in zip(shapes, (low, wide, wide))],
        grid=(1,),
        in_specs=[whole_block(a) for a in arrays],
        out_specs=[fixed_block(s) for s in shapes],
    )(*arrays)


def project_kernel(count, *refs):
    weight, bias, cosine, sine_low, sine_high, rows_out, out = refs[count:]
    part = pl.program_id(0)

    @pl.when(part == 0)
    def _():
        assemble(rows_out, [(r, 0, r.shape[0]) for r in refs[:count]])

    projected = dot(rows_out[...], weight[0], 1, 0) + bias[0].astype(wide)

    @pl.when(part < 2)
    def _():
        scale = jnp.where(part == 0, 0.125, 1.0)
        for j in range(0, projected.shape[1], 128):
            rotated = turned(projected[:, j : j + 128], cosine[...], sine_low[...], sine_high[...])
            out[0, :, j : j + 128] = (rotated * scale).astype(low)

    @pl.when(part == 2)
    def _():
        out[0] = projected.astype(low)


def project(blocks, weight, bias, tables):
    tokens = sum(b.shape[0] for b in blocks)
    _, features, width = weight.shape
    table = whole_block(tables[0])
    return kernel_call(
        partial(project_kernel, len(blocks)),
        6 * tokens * features * width,
        [sds((tokens, features), low), sds((3, tokens, width), low)],
        grid=(3,),
        in_specs=[whole_block(a) for a in blocks]
        + [
            pl.BlockSpec((1, features, width), lambda c: (c, 0, 0)),
            pl.BlockSpec((1, 1, width), lambda c: (c, 0, 0)),
            table,
            table,
            table,
        ],
        out_specs=[fixed_block((tokens, features)), pl.BlockSpec((1, tokens, width), lambda c: (c, 0, 0))],
    )(*blocks, weight, bias, *tables)


def attention_kernel(count, *refs):
    (queries, keys, values, dense, seg_q, place_q, seg_k, place_k, cosine, sine_low, sine_high) = refs[count:-5]
    rows_out, context, out, bias_out, mask = refs[-5:]

    @pl.when(pl.program_id(0) == 0)
    def _():
        assemble(rows_out, [(r, 0, r.shape[0]) for r in refs[:count]])
        allowed = (seg_q[...] == seg_k[...]) & (place_k[...] <= place_q[...])
        mask[...] = jnp.where(allowed, 0.0, masked_score)

    q, k, v = queries[0], keys[0], values[0]
    g = dot(rows_out[...], dense[...], 1, 1, low)
    lane = lax.broadcasted_iota(jnp.int32, q.shape, 1) // HEAD_DIM
    found = []
    for head in range(q.shape[1] // HEAD_DIM):
        mine = lane == head
        scores = dot(jnp.where(mine, q, jnp.zeros_like(q)), k, 1, 1) + mask[...]
        exponent = jnp.exp(scores - jnp.max(scores, -1, keepdims=True))
        soft = exponent * (1.0 / jnp.sum(exponent, -1, keepdims=True))
        soft_low = soft.astype(low)
        prob_grad = dot(jnp.where(mine, g, jnp.zeros_like(g)), v, 1, 1)
        row_dots = jnp.sum(soft * prob_grad, -1, keepdims=True)
        score_grad = (soft * (prob_grad - row_dots)).astype(low)
        found.append(
            (dot(soft_low, v, 1, 0), dot(score_grad, k, 1, 0), dot(score_grad, q, 0, 0), dot(soft_low, g, 0, 0))
        )
    parts = []
    for of_heads in zip(*found):
        chosen = of_heads[0]
        for head, value in enumerate(of_heads[1:], 1):
            chosen = jnp.where(lane == head, value, chosen)
        parts.append(chosen)
    context[...] = parts[0].astype(low)
    back = (cosine[...], -sine_low[...], -sine_high[...])
    turn_back = lambda value: jnp.concatenate(
        [turned(value[:, j : j + 128], *back) for j in range(0, value.shape[1], 128)], 1
    )
    grads = [turn_back(parts[1] * 0.125), turn_back(parts[2]), parts[3]]
    for c, value in enumerate(grads):
        rounded = value.astype(low)
        out[c] = rounded
        bias_out[c] = jnp.sum(rounded.astype(wide), 0, keepdims=True)


def attention(blocks, qkv, dense_weight, seg, place, tables, lanes=LANES):
    _, tokens, width = qkv.shape
    features = dense_weight.shape[1]
    column, row = (lambda a: a.reshape(tokens, 1)), (lambda a: a.reshape(1, tokens))
    extras = [column(seg), column(place), row(seg), row(place), *tables]
    part = lambda c: pl.BlockSpec((1, tokens, lanes), lambda j: (c, 0, j))
    return kernel_call(
        partial(attention_kernel, len(blocks)),
        20 * tokens * tokens * width,
        [
            sds((tokens, features), low),
            sds((tokens, width), low),
            sds((3, tokens, width), low),
            sds((3, 1, width), wide),
        ],
        grid=(width // lanes,),
        in_specs=[whole_block(b) for b in blocks]
        + [part(0), part(1), part(2), pl.BlockSpec((lanes, features), lambda j: (j, 0))]
        + [whole_block(e) for e in extras],
        out_specs=[
            fixed_block((tokens, features)),
            pl.BlockSpec((tokens, lanes), lambda j: (0, j)),
            pl.BlockSpec((3, tokens, lanes), lambda j: (0, 0, j)),
            pl.BlockSpec((3, 1, lanes), lambda j: (0, 0, j)),
        ],
        scratch_shapes=[pltpu.VMEM((tokens, tokens), wide)],
    )(*blocks, qkv, qkv, qkv, dense_weight, *extras)


def outer_pair_kernel(left, right, context, upstream, out):
    count = right.shape[0]
    for c in range(count):
        out[c] = dot(left[...], right[c], 0, 0, low)
    out[count] = dot(context[...], upstream[...], 0, 0, low)


def outer_pair(left, right, context, upstream):
    count, tokens, width = right.shape
    features = left.shape[1]
    columns = pl.BlockSpec((tokens, width), lambda i: (0, i))
    found = kernel_call(
        outer_pair_kernel,
        2 * (count + 1) * tokens * features * width,
        sds((count + 1, features, width), low),
        grid=(features // width,),
        in_specs=[columns, whole_block(right), whole_block(context), columns],
        out_specs=pl.BlockSpec((count + 1, width, width), lambda i: (0, i, 0)),
    )(left, right, context, upstream)
    return found.reshape((count + 1) * features, width)


def widen_pair_kernel(n_first, given, first, second):
    step = pl.program_id(0)

    @pl.when(step < n_first)
    def _():
        first[...] = given[...].astype(wide)

    @pl.when(step >= n_first)
    def _():
        width = given.shape[1]
        for i in range(given.shape[0] // width):
            second[:, i * width : (i + 1) * width] = given[i * width : (i + 1) * width, :].astype(wide)


def widen_pair(given, features, tile=1024):
    rows, width = given.shape
    each = features // tile
    n_first = rows // tile - each
    return kernel_call(
        partial(widen_pair_kernel, n_first),
        rows * width * 256,
        [sds((rows - features, width), wide), sds((width, features), wide)],
        6 * rows * width,
        grid=(n_first + each,),
        in_specs=[pl.BlockSpec((tile, width), lambda s: (s, 0))],
        out_specs=[
            pl.BlockSpec((tile, width), lambda s: (jnp.minimum(s, n_first - 1), 0)),
            pl.BlockSpec((width, tile), lambda s: (0, jnp.maximum(s - n_first, 0))),
        ],
    )(given)


def feed_kernel(layouts, n_arrays, *refs):
    arrays, refs = refs[:n_arrays], refs[n_arrays:]
    up_weight, down_weight, up_bias = refs[:3]
    outs = refs[3:]
    pick = lambda layout: [(arrays[i], first, size) for i, first, size in layout]

    @pl.when(pl.program_id(0) == 0)
    def _():
        for (normed_layout, upstream_layout), (normed_out, upstream_out, *_) in zip(layouts, fives(outs)):
            assemble(normed_out, pick(normed_layout))
            assemble(upstream_out, pick(upstream_layout))

    bias = up_bias[...].astype(wide)
    for normed_out, upstream_out, active_out, grad_out, sum_out in fives(outs):
        active, slope = gelu_and_slope(dot(normed_out[...], up_weight[...], 1, 0) + bias)
        active_out[...] = active.astype(low)
        rounded = (dot(upstream_out[...], down_weight[...], 1, 1) * slope).astype(low)
        grad_out[...] = rounded
        sum_out[...] = jnp.sum(rounded.astype(wide), 0, keepdims=True)


def fives(outs):
    return [outs[i : i + 5] for i in range(0, len(outs), 5)]


def feed(arrays, layouts, up_weight, down_weight, up_bias, tile=512):
    features, hidden = up_weight.shape
    tokens = sum(size for _, _, size in layouts[0][0])
    rows_spec = fixed_block((tokens, features))
    tile_spec = pl.BlockSpec((tokens, tile), lambda j: (0, j))
    sum_spec = pl.BlockSpec((1, tile), lambda j: (0, j))
    shapes = [sds((tokens, features), low)] * 2 + [sds((tokens, hidden), low)] * 2 + [sds((1, hidden), wide)]
    found = kernel_call(
        partial(feed_kernel, layouts, len(arrays)),
        4 * len(layouts) * tokens * features * hidden,
        shapes * len(layouts),
        grid=(hidden // tile,),
        in_specs=[whole_block(a) for a in arrays]
        + [
            pl.BlockSpec((features, tile), lambda j: (0, j)),
            pl.BlockSpec((tile, features), lambda j: (j, 0)),
            pl.BlockSpec((1, tile), lambda j: (0, j)),
        ],
        out_specs=[rows_spec, rows_spec, tile_spec, tile_spec, sum_spec] * len(layouts),
    )(*arrays, up_weight, down_weight, up_bias)
    return fives(found)


def back_kernel(n_tp, active, context, up_grad, part_grad, down, dense, up, part_weight, own, *sent):
    rows = active.shape[0] // n_tp
    mixed = dot(active[...], down[...], 1, 0) + dot(context[...], dense[...], 1, 0)
    normed_grad = dot(up_grad[...], up[...], 1, 1)
    for c in range(3):
        normed_grad = normed_grad + dot(part_grad[c], part_weight[c], 1, 1)
    for i, value in enumerate((mixed, normed_grad)):
        span = slice(i * rows, (i + 1) * rows)
        own[span, :] = value[:rows]
        for r in range(1, n_tp):
            sent[r - 1][span, :] = value[r * rows : (r + 1) * rows].astype(low)


def back_to_tokens(n_tp, active, context, up_grad, part_grad, down, dense, up, part_weight, tile=512):
    tokens, hidden = active.shape
    features, width = down.shape[1], context.shape[1]
    rows = 2 * tokens // n_tp
    column = pl.BlockSpec((rows, tile), lambda j: (0, j))
    return kernel_call(
        partial(back_kernel, n_tp),
        4 * tokens * features * (hidden + 2 * width),
        [sds((rows, features), wide)] + [sds((rows, features), low)] * (n_tp - 1),
        grid=(features // tile,),
        in_specs=[whole_block(a) for a in (active, context, up_grad, part_grad)]
        + [
            pl.BlockSpec((hidden, tile), lambda j: (0, j)),
            pl.BlockSpec((width, tile), lambda j: (0, j)),
            pl.BlockSpec((tile, hidden), lambda j: (j, 0)),
            pl.BlockSpec((3, tile, width), lambda j: (0, j, 0)),
        ],
        out_specs=[column] * n_tp,
    )(active, context, up_grad, part_grad, down, dense, up, part_weight)


def outer_kernel(count, place, *refs):
    out = refs[2 * count]
    for here in range(count):

        @pl.when(place[0] == here)
        def _():
            total = None
            for there in range(count):
                i = here ^ there
                term = dot(refs[i][...], refs[count + i][...], 0, 0)
                total = term if total is None else total + term
            out[...] = total.astype(out.dtype)


def outer_sum(place, lefts, rights, tile_m=512, tile_n=1024):
    count, (tokens, m), n = len(lefts), lefts[0].shape, rights[0].shape[1]
    return kernel_call(
        partial(outer_kernel, count),
        2 * count * tokens * m * n,
        sds((m, n), low),
        grid_spec=pltpu.PrefetchScalarGridSpec(
            num_scalar_prefetch=1,
            grid=(n // tile_n, m // tile_m),
            in_specs=[pl.BlockSpec((tokens, tile_m), lambda j, i, _: (0, i))] * count
            + [pl.BlockSpec((tokens, tile_n), lambda j, i, _: (0, j))] * count,
            out_specs=pl.BlockSpec((tile_m, tile_n), lambda j, i, _: (i, j)),
        ),
    )(place.reshape(1).astype(jnp.int32), *lefts, *rights)


def add_kernel(*refs):
    total = refs[0][...].astype(wide)
    for ref in refs[1:-1]:
        total = total + ref[...].astype(wide)
    refs[-1][...] = total


def added(*terms, tile=512):
    m, n = terms[0].shape
    spec = pl.BlockSpec((tile, n), lambda i: (i, 0))
    return kernel_call(
        add_kernel, m * n * 256, sds((m, n), wide), 8 * m * n, grid=(m // tile,), in_specs=[spec] * len(terms), out_specs=spec
    )(*terms)


def tie(*arrays):
    return lax.optimization_barrier(arrays)


def shards(
    tokens,
    upstream,
    segment_ids,
    positions,
    norm_gain,
    norm_bias,
    qkv_weight,
    qkv_bias,
    dense_weight,
    up_weight,
    up_bias,
    down_weight,
    out_bias,
):
    n_tp, n_line = 4, 4
    dp_place, tp_place = lax.axis_index("dp"), lax.axis_index("tp")
    line_place = dp_place // 2
    rows, features = tokens.shape
    group_rows = rows * n_tp
    heads_wide = qkv_weight.shape[2]
    hidden = up_weight.shape[1]

    def swap_tp(array, flip):
        return lax.ppermute(array, "tp", [(i, i ^ flip) for i in range(n_tp)])

    def swap_core(array):
        return lax.ppermute(array, "dp", [(i, i ^ 1) for i in range(2 * n_line)])

    def swap_line(array, flip):
        return lax.ppermute(array, "dp", [(i, i ^ (2 * flip)) for i in range(2 * n_line)])

    def hop(array, pairs):
        return lax.ppermute(array, "dp", [(2 * s + c, 2 * d + c) for s, d in pairs for c in (0, 1)])

    def to_neighbours(block):
        return swap_tp(block, 1), swap_tp(block, 2)

    def to_diagonal(block_1, block_2):
        size = block_1.shape[0] // 2
        return swap_tp(block_1[:size], 2), swap_tp(block_2[size:], 1)

    def from_others(array):
        return [swap_tp(array, r) for r in range(1, n_tp)]

    gain, shift, last_bias = (a.reshape(1, features) for a in (norm_gain, norm_bias, out_bias))
    normed, both = norm_rows(tokens, upstream, gain, shift)
    normed_blocks = [normed, *from_others(normed)]
    above_1, below_1 = hop(both, [(0, 1), (1, 2), (2, 3)]), hop(both, [(1, 0), (2, 1), (3, 2)])

    by_owner = jnp.stack([segment_ids.reshape(n_tp, rows), positions.reshape(n_tp, rows)])
    owner = tp_place ^ jnp.arange(n_tp)
    pick = (owner[:, None] == jnp.arange(n_tp)[None, :]).astype(jnp.int32)
    arranged = jnp.sum(pick[None, :, :, None] * by_owner[:, None, :, :], 2).reshape(2, group_rows)
    seg, place = arranged[0], arranged[1]
    cosine_table, sine_table = rotary_tables(place, ROT)
    cosine, sine = cosine_table[:, 0, :], sine_table[:, 0, :]
    still = jnp.zeros((group_rows, HEAD_DIM - ROT), wide)
    quiet = jnp.zeros((group_rows, ROT // 2), wide)
    tables = [
        jnp.concatenate([cosine, still + 1.0], 1),
        jnp.concatenate([-sine[:, : ROT // 2], quiet, still], 1),
        jnp.concatenate([quiet, sine[:, : ROT // 2], still], 1),
    ]
    tables = [jnp.concatenate([t] * (128 // HEAD_DIM), 1) for t in tables]
    parts_weight = qkv_weight.transpose(1, 0, 2)
    parts_bias = qkv_bias.reshape(3, 1, heads_wide)

    normed_blocks, tables, seg, place, late_upstream = tie(normed_blocks, tables, seg, place, upstream)
    upstream_r1, upstream_r2 = to_neighbours(late_upstream)
    group_normed, qkv = project(normed_blocks, parts_weight, parts_bias, tables)

    group_normed, qkv, upstream_r1, upstream_r2, above_1, below_1 = tie(
        group_normed, qkv, upstream_r1, upstream_r2, above_1, below_1
    )
    upstream_r3 = to_diagonal(upstream_r1, upstream_r2)
    above_2, below_2 = hop(above_1, [(1, 2), (2, 3)]), hop(below_1, [(1, 0), (2, 1)])
    slot_1 = jnp.where(line_place % 2 == 1, above_1, below_1)
    upstream_r3, slot_1 = tie(upstream_r3, slot_1)
    slot_1_r1, slot_1_r2 = to_neighbours(slot_1)
    upstream_blocks = [upstream, upstream_r1, upstream_r2, *upstream_r3]
    group_upstream, context, projected_grad, qkv_bias_grad = attention(
        upstream_blocks, qkv, dense_weight, seg, place, tables
    )

    slot_1_r1, slot_1_r2, above_2, below_2, group_upstream, context, projected_grad = tie(
        slot_1_r1, slot_1_r2, above_2, below_2, group_upstream, context, projected_grad
    )
    above_3, below_3 = hop(above_2, [(2, 3)]), hop(below_2, [(1, 0)])
    slot_1_r3 = to_diagonal(slot_1_r1, slot_1_r2)
    slot_2 = jnp.where(line_place >= 2, above_2, below_2)
    pair_part = outer_pair(group_normed, projected_grad, context, group_upstream)

    slot_layout = (
        [(0, 0, rows), (1, 0, rows), (2, 0, rows), (3, 0, rows)],
        [(0, rows, rows), (1, rows, rows), (2, rows, rows), (4, 0, rows)],
    )
    own_layout = ([(0, 0, group_rows)], [(1, 0, group_rows)])
    weights = (up_weight, down_weight, up_bias.reshape(1, hidden))
    group_normed, group_upstream, context, projected_grad, pair_part, above_3, below_3, slot_1_r3 = tie(
        group_normed, group_upstream, context, projected_grad, pair_part, above_3, below_3, slot_1_r3
    )
    slot_2_r1, slot_2_r2 = to_neighbours(slot_2)
    pair_share = lax.psum_scatter(pair_part, "dp", scatter_dimension=0, tiled=True)
    (group_0,) = feed([group_normed, group_upstream], [own_layout], *weights)
    (group_1,) = feed([slot_1, slot_1_r1, slot_1_r2, *slot_1_r3], [slot_layout], *weights)

    slot_2_r1, slot_2_r2, group_0, group_1 = tie(slot_2_r1, slot_2_r2, group_0, group_1)
    slot_3 = jnp.where(
        line_place == 0, below_3, jnp.where(line_place == 1, below_1, jnp.where(line_place == 2, above_1, above_3))
    )
    slot_2_r3 = to_diagonal(slot_2_r1, slot_2_r2)
    slot_3_r1, slot_3_r2 = to_neighbours(slot_3)
    active, up_input_grad, up_bias_grad = group_0[2:]
    own_part, *parts = back_to_tokens(
        n_tp, active, context, up_input_grad, projected_grad, down_weight, dense_weight, up_weight, parts_weight
    )

    slot_2_r3, own_part, parts, slot_3_r1, slot_3_r2 = tie(slot_2_r3, own_part, parts, slot_3_r1, slot_3_r2)
    slot_3_r3 = to_diagonal(slot_3_r1, slot_3_r2)
    (group_2,) = feed([slot_2, slot_2_r1, slot_2_r2, *slot_2_r3], [slot_layout], *weights)

    slot_3_r3, parts, group_2 = tie(slot_3_r3, parts, group_2)
    got = [swap_tp(part, r + 1) for r, part in enumerate(parts)]
    (group_3,) = feed([slot_3, slot_3_r1, slot_3_r2, *slot_3_r3], [slot_layout], *weights)

    group_3, pair_share = tie(group_3, pair_share)
    pair_sum = lax.all_gather(pair_share, "dp", axis=0, tiled=True)

    groups = [group_0, group_1, group_2, group_3]
    normeds, upstreams, actives, up_grads = ([g[i] for g in groups] for i in range(4))
    up_part = outer_sum(line_place, normeds, up_grads)
    up_part, actives, upstreams = tie(up_part, list(actives), list(upstreams))
    other_up_part = swap_core(up_part)
    down_part = outer_sum(line_place, actives, upstreams)
    got, own_part, down_part = tie(got, own_part, down_part)
    other_down_part = swap_core(down_part)
    mixed, input_grad, sums = norm_back(tokens, upstream, gain, last_bias, own_part, *got)
    turn = swap_tp(sums, 1)
    up_weight_grad = added(up_part, other_up_part)
    turn, up_weight_grad = tie(turn, up_weight_grad)
    sums = sums + turn
    turn = swap_tp(sums, 2)
    down_weight_grad = added(down_part, other_down_part)
    turn, down_weight_grad, pair_sum = tie(turn, down_weight_grad, pair_sum)
    sums = sums + turn
    small = jnp.concatenate([sums.reshape(1, -1), qkv_bias_grad.reshape(1, -1), up_bias_grad], 1)
    turn = swap_core(small)
    qkv_weight_grad, dense_weight_grad = widen_pair(pair_sum, features)
    qkv_weight_grad = qkv_weight_grad.reshape(3, features, heads_wide).transpose(1, 0, 2)
    turn, qkv_weight_grad = tie(turn, qkv_weight_grad)
    small = small + turn
    turns = [swap_line(small, k) for k in range(1, n_line)]
    small = ((small + turns[0]) + (turns[1] + turns[2]))[0]
    norm_gain_grad = small[:features]
    norm_bias_grad = small[features : 2 * features]
    out_bias_grad = small[2 * features : 3 * features]
    qkv_bias_grad = small[3 * features : 3 * features + 3 * heads_wide].reshape(3, heads_wide)
    up_bias_grad = small[3 * features + 3 * heads_wide :]

    return (
        mixed,
        input_grad,
        norm_gain_grad,
        norm_bias_grad,
        qkv_weight_grad,
        qkv_bias_grad,
        dense_weight_grad,
        up_weight_grad,
        up_bias_grad,
        down_weight_grad,
        out_bias_grad,
    )


def allowed_block(segment_ids, positions, begin_row, block_rows):
    seg_rows = lax.dynamic_slice_in_dim(segment_ids, begin_row, block_rows)
    place_rows = lax.dynamic_slice_in_dim(positions, begin_row, block_rows)
    return (seg_rows[:, None] == segment_ids[None, :]) & (positions[None, :] <= place_rows[:, None])


def block_scores(query_block, keys_low, allowed):
    scores = (
        jnp.einsum("qhe,khe->hqk", query_block, keys_low, preferred_element_type=jnp.float32)
        * 0.125
    )
    return jnp.where(allowed[None], scores, masked_score)


def up_projection(gathered, up_weight, up_bias):
    up_input = jnp.dot(gathered, up_weight, preferred_element_type=jnp.float32) + up_bias.astype(
        jnp.float32
    )
    return (up_input, jax.nn.gelu(up_input, approximate=True).astype(jnp.bfloat16))


def row_product(left, right):
    return jnp.dot(left, right, preferred_element_type=jnp.float32)


def general_shards(
    tokens,
    upstream,
    segment_ids,
    positions,
    norm_gain,
    norm_bias,
    qkv_weight,
    qkv_bias,
    dense_weight,
    up_weight,
    up_bias,
    down_weight,
    out_bias,
):
    head_count = qkv_weight.shape[2] // HEAD_DIM
    inputs = tokens.astype(jnp.float32)
    normed_low = layer_norm(inputs, norm_gain, norm_bias).astype(jnp.bfloat16)
    gathered = lax.all_gather(normed_low, "tp", axis=0, tiled=True)
    group_rows = gathered.shape[0]
    block_rows = math.gcd(group_rows, 512)
    block_count = group_rows // block_rows
    projected = (
        jnp.einsum("td,dch->tch", gathered, qkv_weight, preferred_element_type=jnp.float32)
        + qkv_bias.astype(jnp.float32)[None]
    )
    head_shape = (group_rows, head_count, HEAD_DIM)
    cosine_table, sine_table = rotary_tables(positions, ROT)
    queries = rotate(projected[:, 0].reshape(head_shape), cosine_table, sine_table).astype(
        jnp.bfloat16
    )
    keys_low = rotate(projected[:, 1].reshape(head_shape), cosine_table, sine_table).astype(
        jnp.bfloat16
    )
    values_low = projected[:, 2].reshape(head_shape).astype(jnp.bfloat16)

    def forward_block(block_index):
        begin_row = block_index * block_rows
        query_block = lax.dynamic_slice_in_dim(queries, begin_row, block_rows, 0)
        scores = block_scores(
            query_block, keys_low, allowed_block(segment_ids, positions, begin_row, block_rows)
        )
        highest_score = jnp.max(scores, -1, keepdims=True)
        exponent = jnp.exp(scores - highest_score)
        totals = jnp.sum(exponent, -1, keepdims=True)
        soft_low = (exponent / totals).astype(jnp.bfloat16)
        context_block = jnp.einsum(
            "hqk,khe->qhe", soft_low, values_low, preferred_element_type=jnp.float32
        )
        return (context_block.astype(jnp.bfloat16), highest_score + jnp.log(totals))

    context_blocks, log_blocks = lax.map(forward_block, jnp.arange(block_count, dtype=jnp.int32))
    context_low = context_blocks.reshape(group_rows, head_count * HEAD_DIM)
    up_input, up_active_low = up_projection(gathered, up_weight, up_bias)
    summed = lax.psum_scatter(
        row_product(context_low, dense_weight) + row_product(up_active_low, down_weight),
        "tp",
        scatter_dimension=0,
        tiled=True,
    )
    mixed = (inputs + summed + out_bias).astype(jnp.bfloat16)
    upstream_all = lax.all_gather(upstream, "tp", axis=0, tiled=True)
    unit_column = jnp.ones((group_rows,), jnp.bfloat16)
    out_bias_grad = jnp.einsum(
        "t,td->d", unit_column, upstream_all, preferred_element_type=jnp.float32
    )
    dense_weight_grad = jnp.einsum(
        "te,td->ed", context_low, upstream_all, preferred_element_type=jnp.float32
    )
    down_weight_grad = jnp.einsum(
        "tf,td->fd", up_active_low, upstream_all, preferred_element_type=jnp.float32
    )
    context_grad = jnp.einsum(
        "td,ed->te", upstream_all, dense_weight, preferred_element_type=jnp.float32
    )
    context_grad_low = context_grad.astype(jnp.bfloat16).reshape(head_shape)
    active_grad = jnp.einsum(
        "td,fd->tf", upstream_all, down_weight, preferred_element_type=jnp.float32
    )
    _, gelu_back = jax.vjp(partial(jax.nn.gelu, approximate=True), up_input)
    up_input_grad = gelu_back(active_grad)[0].astype(jnp.bfloat16)
    up_bias_grad = jnp.einsum(
        "t,tf->f", unit_column, up_input_grad, preferred_element_type=jnp.float32
    )

    def backward_block(running, block_index):
        key_grad, value_grad = running
        begin_row = block_index * block_rows
        query_block = lax.dynamic_slice_in_dim(queries, begin_row, block_rows, 0)
        output_grad = lax.dynamic_slice_in_dim(context_grad_low, begin_row, block_rows, 0)
        log_totals = lax.dynamic_index_in_dim(log_blocks, block_index, 0, keepdims=False)
        scores = block_scores(
            query_block, keys_low, allowed_block(segment_ids, positions, begin_row, block_rows)
        )
        attn_soft = jnp.exp(scores - log_totals)
        value_grad = value_grad + jnp.einsum(
            "hqk,qhe->khe",
            attn_soft.astype(jnp.bfloat16),
            output_grad,
            preferred_element_type=jnp.float32,
        )
        prob_grad = jnp.einsum(
            "qhe,khe->hqk", output_grad, values_low, preferred_element_type=jnp.float32
        )
        row_dots = jnp.sum(attn_soft * prob_grad, -1, keepdims=True)
        score_grad = (attn_soft * (prob_grad - row_dots)).astype(jnp.bfloat16)
        query_grad = (
            jnp.einsum("hqk,khe->qhe", score_grad, keys_low, preferred_element_type=jnp.float32)
            * 0.125
        )
        key_grad = (
            key_grad
            + jnp.einsum(
                "hqk,qhe->khe", score_grad, query_block, preferred_element_type=jnp.float32
            )
            * 0.125
        )
        return ((key_grad, value_grad), query_grad)

    empty_grad = jnp.zeros(head_shape, jnp.float32)
    (key_grad, value_grad), query_blocks = lax.scan(
        backward_block, (empty_grad, empty_grad), jnp.arange(block_count, dtype=jnp.int32)
    )
    query_grad = query_blocks.reshape(head_shape)
    projected_grad = jnp.stack(
        [
            rotate(query_grad, cosine_table, -sine_table),
            rotate(key_grad, cosine_table, -sine_table),
            value_grad,
        ],
        axis=1,
    )
    projected_grad = projected_grad.reshape(group_rows, 3, head_count * HEAD_DIM).astype(
        jnp.bfloat16
    )
    qkv_bias_grad = jnp.einsum(
        "t,tch->ch", unit_column, projected_grad, preferred_element_type=jnp.float32
    )
    qkv_weight_grad = jnp.einsum(
        "td,tch->dch", gathered, projected_grad, preferred_element_type=jnp.float32
    )
    up_weight_grad = jnp.einsum(
        "td,tf->df", gathered, up_input_grad, preferred_element_type=jnp.float32
    )
    first = jnp.einsum(
        "tch,dch->td", projected_grad, qkv_weight, preferred_element_type=jnp.float32
    )
    normed_grad = lax.psum_scatter(
        first
        + jnp.einsum("tf,df->td", up_input_grad, up_weight, preferred_element_type=jnp.float32),
        "tp",
        scatter_dimension=0,
        tiled=True,
    )
    _, norm_back = jax.vjp(layer_norm, inputs, norm_gain, norm_bias)
    input_part, gain_part, shift_part = norm_back(normed_grad)
    input_grad = upstream.astype(jnp.float32) + input_part
    norm_gain_grad, norm_bias_grad = lax.psum((gain_part, shift_part), ("dp", "tp"))
    (
        qkv_weight_grad,
        qkv_bias_grad,
        dense_weight_grad,
        up_weight_grad,
        up_bias_grad,
        down_weight_grad,
        out_bias_grad,
    ) = lax.psum(
        (
            qkv_weight_grad,
            qkv_bias_grad,
            dense_weight_grad,
            up_weight_grad,
            up_bias_grad,
            down_weight_grad,
            out_bias_grad,
        ),
        "dp",
    )
    return (
        mixed,
        input_grad,
        norm_gain_grad,
        norm_bias_grad,
        qkv_weight_grad,
        qkv_bias_grad,
        dense_weight_grad,
        up_weight_grad,
        up_bias_grad,
        down_weight_grad,
        out_bias_grad,
    )


def solution(mesh):
    fits = mesh.shape["dp"] == 8 and mesh.shape["tp"] == 4
    return jax.shard_map(
        shards if fits else general_shards,
        mesh=mesh,
        in_specs=(
            P(("dp", "tp"), None),
            P(("dp", "tp"), None),
            P("dp"),
            P("dp"),
            P(),
            P(),
            P(None, None, "tp"),
            P(None, "tp"),
            P("tp", None),
            P(None, "tp"),
            P("tp"),
            P("tp", None),
            P(),
        ),
        out_specs=(
            P(("dp", "tp"), None),
            P(("dp", "tp"), None),
            P(),
            P(),
            P(None, None, "tp"),
            P(None, "tp"),
            P("tp", None),
            P(None, "tp"),
            P("tp"),
            P("tp", None),
            P(),
        ),
        check_vma=False,
    )
```

```python
from functools import partial
import math

import jax
import jax.numpy as jnp
from jax import lax
from jax.experimental import pallas as pl
from jax.experimental.pallas import tpu as pltpu
from jax.sharding import PartitionSpec as P

HEAD_DIM = 64
ROT = 32
norm_epsilon = 1e-05
masked_score = -1e30
low = jnp.bfloat16
wide = jnp.float32
VMEM = 56 * 2**20
HASTE = 0.02
LANES = 256


def dot(left, right, left_dim, right_dim, kind=wide):
    return lax.dot_general(
        left, right, (((left_dim,), (right_dim,)), ((), ())), preferred_element_type=wide
    ).astype(kind)


def layer_norm(values, gain, shift):
    averaged = jnp.mean(values, -1, keepdims=True)
    centred = values - averaged
    spread = jnp.mean(centred * centred, -1, keepdims=True)
    return centred * lax.rsqrt(spread + norm_epsilon) * gain + shift


def rotary_tables(places, rot_dims):
    half_rot = rot_dims // 2
    frequency = jnp.power(10000.0, -2.0 * jnp.arange(half_rot).astype(wide) / rot_dims)
    phases = places.astype(wide)[:, None] * frequency[None, :]
    cosine_table = jnp.concatenate([jnp.cos(phases), jnp.cos(phases)], -1)[:, None, :]
    sine_table = jnp.concatenate([jnp.sin(phases), jnp.sin(phases)], -1)[:, None, :]
    return (cosine_table, sine_table)


def rotate(values, cosine_table, sine_table):
    rot_dims = cosine_table.shape[-1]
    half_rot = rot_dims // 2
    rotated_part = values[..., :rot_dims]
    turned = jnp.concatenate([-rotated_part[..., half_rot:], rotated_part[..., :half_rot]], -1)
    return jnp.concatenate(
        [rotated_part * cosine_table + turned * sine_table, values[..., rot_dims:]], -1
    )


def gelu_and_slope(v):
    square = v * v
    inner = jnp.tanh(v * (0.7978845608 + 0.035677408137 * square))
    half = 0.5 + 0.5 * inner
    slope = half + (v - v * (inner * inner)) * (0.3989422804 + 0.0535161122 * square)
    return v * half, slope


def kernel_call(body, flops, out_shape, traffic=0, **kinds):
    return pl.pallas_call(
        body,
        out_shape=out_shape,
        compiler_params=pltpu.CompilerParams(vmem_limit_bytes=VMEM),
        cost_estimate=pl.CostEstimate(
            flops=int(flops * HASTE), bytes_accessed=traffic + int(flops * HASTE) // 512, transcendentals=0
        ),
        **kinds,
    )


def sds(shape, kind):
    return jax.ShapeDtypeStruct(shape, kind)


def whole_block(array):
    zeros = (0,) * array.ndim
    return pl.BlockSpec(array.shape, lambda *_: zeros, pipeline_mode=pl.Buffered(1))


def fixed_block(shape):
    zeros = (0,) * len(shape)
    return pl.BlockSpec(shape, lambda *_: zeros)


def assemble(target, pieces):
    at = 0
    for ref, first, size in pieces:
        target[at : at + size, :] = ref[first : first + size, :]
        at += size


def turned(values, cosine, sine_low, sine_high):
    return (
        values * cosine
        + pltpu.roll(values, 128 - ROT // 2, 1) * sine_low
        + pltpu.roll(values, ROT // 2, 1) * sine_high
    )


def row_means(inputs):
    centred = inputs - jnp.mean(inputs, -1, keepdims=True)
    spread = jnp.mean(centred * centred, -1, keepdims=True)
    scale = lax.rsqrt(spread + norm_epsilon)
    return centred * scale, scale


def norm_kernel(tokens, upstream, gain, shift, normed, both):
    unit, _ = row_means(tokens[...].astype(wide))
    rows = tokens.shape[0]
    normed[...] = (unit * gain[...] + shift[...]).astype(low)
    both[:rows, :] = normed[...]
    both[rows:, :] = upstream[...]


def norm_rows(tokens, upstream, gain, shift):
    rows, features = tokens.shape
    arrays = [tokens, upstream, gain, shift]
    return kernel_call(
        norm_kernel,
        rows * features * 512,
        [sds((rows, features), low), sds((2 * rows, features), low)],
        grid=(1,),
        in_specs=[whole_block(a) for a in arrays],
        out_specs=[fixed_block((rows, features)), fixed_block((2 * rows, features))],
    )(*arrays)


def norm_back_kernel(tokens, upstream, gain, out_bias, own, got_1, got_2, got_3, mixed, input_grad, sums):
    rows = tokens.shape[0]
    inputs, cotangent = tokens[...].astype(wide), upstream[...].astype(wide)

    def total(first):
        span = slice(first, first + rows)
        return (own[span, :] + got_1[span, :].astype(wide)) + (
            got_2[span, :].astype(wide) + got_3[span, :].astype(wide)
        )

    mixed[...] = (inputs + total(0) + out_bias[...]).astype(low)
    unit, scale = row_means(inputs)
    normed_grad = total(rows)
    e = normed_grad * gain[...]
    along = jnp.mean(e * unit, -1, keepdims=True)
    input_grad[...] = cotangent + (e - jnp.mean(e, -1, keepdims=True) - unit * along) * scale
    sums[0:1, :] = jnp.sum(normed_grad * unit, 0, keepdims=True)
    sums[1:2, :] = jnp.sum(normed_grad, 0, keepdims=True)
    sums[2:3, :] = jnp.sum(cotangent, 0, keepdims=True)


def norm_back(*arrays):
    rows, features = arrays[0].shape
    shapes = [(rows, features), (rows, features), (3, features)]
    return kernel_call(
        norm_back_kernel,
        rows * features * 1024,
        [sds(s, k) for s, k in zip(shapes, (low, wide, wide))],
        grid=(1,),
        in_specs=[whole_block(a) for a in arrays],
        out_specs=[fixed_block(s) for s in shapes],
    )(*arrays)


def project_kernel(count, *refs):
    weight, bias, cosine, sine_low, sine_high, rows_out, out = refs[count:]
    part = pl.program_id(0)

    @pl.when(part == 0)
    def _():
        assemble(rows_out, [(r, 0, r.shape[0]) for r in refs[:count]])

    projected = dot(rows_out[...], weight[0], 1, 0) + bias[0].astype(wide)

    @pl.when(part < 2)
    def _():
        scale = jnp.where(part == 0, 0.125, 1.0)
        for j in range(0, projected.shape[1], 128):
            rotated = turned(projected[:, j : j + 128], cosine[...], sine_low[...], sine_high[...])
            out[0, :, j : j + 128] = (rotated * scale).astype(low)

    @pl.when(part == 2)
    def _():
        out[0] = projected.astype(low)


def project(blocks, weight, bias, tables):
    tokens = sum(b.shape[0] for b in blocks)
    _, features, width = weight.shape
    table = whole_block(tables[0])
    return kernel_call(
        partial(project_kernel, len(blocks)),
        6 * tokens * features * width,
        [sds((tokens, features), low), sds((3, tokens, width), low)],
        grid=(3,),
        in_specs=[whole_block(a) for a in blocks]
        + [
            pl.BlockSpec((1, features, width), lambda c: (c, 0, 0)),
            pl.BlockSpec((1, 1, width), lambda c: (c, 0, 0)),
            table,
            table,
            table,
        ],
        out_specs=[fixed_block((tokens, features)), pl.BlockSpec((1, tokens, width), lambda c: (c, 0, 0))],
    )(*blocks, weight, bias, *tables)


def attention_kernel(count, *refs):
    (queries, keys, values, dense, seg_q, place_q, seg_k, place_k, cosine, sine_low, sine_high) = refs[count:-5]
    rows_out, context, out, bias_out, mask = refs[-5:]

    @pl.when(pl.program_id(0) == 0)
    def _():
        assemble(rows_out, [(r, 0, r.shape[0]) for r in refs[:count]])
        allowed = (seg_q[...] == seg_k[...]) & (place_k[...] <= place_q[...])
        mask[...] = jnp.where(allowed, 0.0, masked_score)

    q, k, v = queries[0], keys[0], values[0]
    g = dot(rows_out[...], dense[...], 1, 1, low)
    lane = lax.broadcasted_iota(jnp.int32, q.shape, 1) // HEAD_DIM
    found = []
    for head in range(q.shape[1] // HEAD_DIM):
        mine = lane == head
        scores = dot(jnp.where(mine, q, jnp.zeros_like(q)), k, 1, 1) + mask[...]
        exponent = jnp.exp(scores - jnp.max(scores, -1, keepdims=True))
        soft = exponent * (1.0 / jnp.sum(exponent, -1, keepdims=True))
        soft_low = soft.astype(low)
        prob_grad = dot(jnp.where(mine, g, jnp.zeros_like(g)), v, 1, 1)
        row_dots = jnp.sum(soft * prob_grad, -1, keepdims=True)
        score_grad = (soft * (prob_grad - row_dots)).astype(low)
        found.append(
            (dot(soft_low, v, 1, 0), dot(score_grad, k, 1, 0), dot(score_grad, q, 0, 0), dot(soft_low, g, 0, 0))
        )
    parts = []
    for of_heads in zip(*found):
        chosen = of_heads[0]
        for head, value in enumerate(of_heads[1:], 1):
            chosen = jnp.where(lane == head, value, chosen)
        parts.append(chosen)
    context[...] = parts[0].astype(low)
    back = (cosine[...], -sine_low[...], -sine_high[...])
    turn_back = lambda value: jnp.concatenate(
        [turned(value[:, j : j + 128], *back) for j in range(0, value.shape[1], 128)], 1
    )
    grads = [turn_back(parts[1] * 0.125), turn_back(parts[2]), parts[3]]
    for c, value in enumerate(grads):
        rounded = value.astype(low)
        out[c] = rounded
        bias_out[c] = jnp.sum(rounded.astype(wide), 0, keepdims=True)


def attention(blocks, qkv, dense_weight, seg, place, tables, lanes=LANES):
    _, tokens, width = qkv.shape
    features = dense_weight.shape[1]
    column, row = (lambda a: a.reshape(tokens, 1)), (lambda a: a.reshape(1, tokens))
    extras = [column(seg), column(place), row(seg), row(place), *tables]
    part = lambda c: pl.BlockSpec((1, tokens, lanes), lambda j: (c, 0, j))
    return kernel_call(
        partial(attention_kernel, len(blocks)),
        20 * tokens * tokens * width,
        [
            sds((tokens, features), low),
            sds((tokens, width), low),
            sds((3, tokens, width), low),
            sds((3, 1, width), wide),
        ],
        grid=(width // lanes,),
        in_specs=[whole_block(b) for b in blocks]
        + [part(0), part(1), part(2), pl.BlockSpec((lanes, features), lambda j: (j, 0))]
        + [whole_block(e) for e in extras],
        out_specs=[
            fixed_block((tokens, features)),
            pl.BlockSpec((tokens, lanes), lambda j: (0, j)),
            pl.BlockSpec((3, tokens, lanes), lambda j: (0, 0, j)),
            pl.BlockSpec((3, 1, lanes), lambda j: (0, 0, j)),
        ],
        scratch_shapes=[pltpu.VMEM((tokens, tokens), wide)],
    )(*blocks, qkv, qkv, qkv, dense_weight, *extras)


def outer_pair_kernel(left, right, context, upstream, out):
    count = right.shape[0]
    for c in range(count):
        out[c] = dot(left[...], right[c], 0, 0, low)
    out[count] = dot(context[...], upstream[...], 0, 0, low)


def outer_pair(left, right, context, upstream):
    count, tokens, width = right.shape
    features = left.shape[1]
    columns = pl.BlockSpec((tokens, width), lambda i: (0, i))
    found = kernel_call(
        outer_pair_kernel,
        2 * (count + 1) * tokens * features * width,
        sds((count + 1, features, width), low),
        grid=(features // width,),
        in_specs=[columns, whole_block(right), whole_block(context), columns],
        out_specs=pl.BlockSpec((count + 1, width, width), lambda i: (0, i, 0)),
    )(left, right, context, upstream)
    return found.reshape((count + 1) * features, width)


def widen_pair_kernel(n_first, given, first, second):
    step = pl.program_id(0)

    @pl.when(step < n_first)
    def _():
        first[...] = given[...].astype(wide)

    @pl.when(step >= n_first)
    def _():
        width = given.shape[1]
        for i in range(given.shape[0] // width):
            second[:, i * width : (i + 1) * width] = given[i * width : (i + 1) * width, :].astype(wide)


def widen_pair(given, features, tile=1024):
    rows, width = given.shape
    each = features // tile
    n_first = rows // tile - each
    return kernel_call(
        partial(widen_pair_kernel, n_first),
        rows * width * 256,
        [sds((rows - features, width), wide), sds((width, features), wide)],
        6 * rows * width,
        grid=(n_first + each,),
        in_specs=[pl.BlockSpec((tile, width), lambda s: (s, 0))],
        out_specs=[
            pl.BlockSpec((tile, width), lambda s: (jnp.minimum(s, n_first - 1), 0)),
            pl.BlockSpec((width, tile), lambda s: (0, jnp.maximum(s - n_first, 0))),
        ],
    )(given)


def feed_kernel(layouts, n_arrays, *refs):
    arrays, refs = refs[:n_arrays], refs[n_arrays:]
    up_weight, down_weight, up_bias = refs[:3]
    outs = refs[3:]
    pick = lambda layout: [(arrays[i], first, size) for i, first, size in layout]

    @pl.when(pl.program_id(0) == 0)
    def _():
        for (normed_layout, upstream_layout), (normed_out, upstream_out, *_) in zip(layouts, fives(outs)):
            assemble(normed_out, pick(normed_layout))
            assemble(upstream_out, pick(upstream_layout))

    bias = up_bias[...].astype(wide)
    for normed_out, upstream_out, active_out, grad_out, sum_out in fives(outs):
        active, slope = gelu_and_slope(dot(normed_out[...], up_weight[...], 1, 0) + bias)
        active_out[...] = active.astype(low)
        rounded = (dot(upstream_out[...], down_weight[...], 1, 1) * slope).astype(low)
        grad_out[...] = rounded
        sum_out[...] = jnp.sum(rounded.astype(wide), 0, keepdims=True)


def fives(outs):
    return [outs[i : i + 5] for i in range(0, len(outs), 5)]


def feed(arrays, layouts, up_weight, down_weight, up_bias, tile=512):
    features, hidden = up_weight.shape
    tokens = sum(size for _, _, size in layouts[0][0])
    rows_spec = fixed_block((tokens, features))
    tile_spec = pl.BlockSpec((tokens, tile), lambda j: (0, j))
    sum_spec = pl.BlockSpec((1, tile), lambda j: (0, j))
    shapes = [sds((tokens, features), low)] * 2 + [sds((tokens, hidden), low)] * 2 + [sds((1, hidden), wide)]
    found = kernel_call(
        partial(feed_kernel, layouts, len(arrays)),
        4 * len(layouts) * tokens * features * hidden,
        shapes * len(layouts),
        grid=(hidden // tile,),
        in_specs=[whole_block(a) for a in arrays]
        + [
            pl.BlockSpec((features, tile), lambda j: (0, j)),
            pl.BlockSpec((tile, features), lambda j: (j, 0)),
            pl.BlockSpec((1, tile), lambda j: (0, j)),
        ],
        out_specs=[rows_spec, rows_spec, tile_spec, tile_spec, sum_spec] * len(layouts),
    )(*arrays, up_weight, down_weight, up_bias)
    return fives(found)


def back_kernel(n_tp, active, context, up_grad, part_grad, down, dense, up, part_weight, own, *sent):
    rows = active.shape[0] // n_tp
    mixed = dot(active[...], down[...], 1, 0) + dot(context[...], dense[...], 1, 0)
    normed_grad = dot(up_grad[...], up[...], 1, 1)
    for c in range(3):
        normed_grad = normed_grad + dot(part_grad[c], part_weight[c], 1, 1)
    for i, value in enumerate((mixed, normed_grad)):
        span = slice(i * rows, (i + 1) * rows)
        own[span, :] = value[:rows]
        for r in range(1, n_tp):
            sent[r - 1][span, :] = value[r * rows : (r + 1) * rows].astype(low)


def back_to_tokens(n_tp, active, context, up_grad, part_grad, down, dense, up, part_weight, tile=512):
    tokens, hidden = active.shape
    features, width = down.shape[1], context.shape[1]
    rows = 2 * tokens // n_tp
    column = pl.BlockSpec((rows, tile), lambda j: (0, j))
    return kernel_call(
        partial(back_kernel, n_tp),
        4 * tokens * features * (hidden + 2 * width),
        [sds((rows, features), wide)] + [sds((rows, features), low)] * (n_tp - 1),
        grid=(features // tile,),
        in_specs=[whole_block(a) for a in (active, context, up_grad, part_grad)]
        + [
            pl.BlockSpec((hidden, tile), lambda j: (0, j)),
            pl.BlockSpec((width, tile), lambda j: (0, j)),
            pl.BlockSpec((tile, hidden), lambda j: (j, 0)),
            pl.BlockSpec((3, tile, width), lambda j: (0, j, 0)),
        ],
        out_specs=[column] * n_tp,
    )(active, context, up_grad, part_grad, down, dense, up, part_weight)


def outer_kernel(count, place, *refs):
    out = refs[2 * count]
    for here in range(count):

        @pl.when(place[0] == here)
        def _():
            total = None
            for there in range(count):
                i = here ^ there
                term = dot(refs[i][...], refs[count + i][...], 0, 0)
                total = term if total is None else total + term
            out[...] = total.astype(out.dtype)


def outer_sum(place, lefts, rights, tile_m=512, tile_n=1024):
    count, (tokens, m), n = len(lefts), lefts[0].shape, rights[0].shape[1]
    return kernel_call(
        partial(outer_kernel, count),
        2 * count * tokens * m * n,
        sds((m, n), low),
        grid_spec=pltpu.PrefetchScalarGridSpec(
            num_scalar_prefetch=1,
            grid=(n // tile_n, m // tile_m),
            in_specs=[pl.BlockSpec((tokens, tile_m), lambda j, i, _: (0, i))] * count
            + [pl.BlockSpec((tokens, tile_n), lambda j, i, _: (0, j))] * count,
            out_specs=pl.BlockSpec((tile_m, tile_n), lambda j, i, _: (i, j)),
        ),
    )(place.reshape(1).astype(jnp.int32), *lefts, *rights)


def add_kernel(*refs):
    total = refs[0][...].astype(wide)
    for ref in refs[1:-1]:
        total = total + ref[...].astype(wide)
    refs[-1][...] = total


def added(*terms, tile=512):
    m, n = terms[0].shape
    spec = pl.BlockSpec((tile, n), lambda i: (i, 0))
    return kernel_call(
        add_kernel, m * n * 256, sds((m, n), wide), 8 * m * n, grid=(m // tile,), in_specs=[spec] * len(terms), out_specs=spec
    )(*terms)


def tie(*arrays):
    return lax.optimization_barrier(arrays)


def shards(
    tokens,
    upstream,
    segment_ids,
    positions,
    norm_gain,
    norm_bias,
    qkv_weight,
    qkv_bias,
    dense_weight,
    up_weight,
    up_bias,
    down_weight,
    out_bias,
):
    n_tp, n_line = 4, 4
    dp_place, tp_place = lax.axis_index("dp"), lax.axis_index("tp")
    line_place = dp_place // 2
    rows, features = tokens.shape
    group_rows = rows * n_tp
    heads_wide = qkv_weight.shape[2]
    hidden = up_weight.shape[1]

    def swap_tp(array, flip):
        return lax.ppermute(array, "tp", [(i, i ^ flip) for i in range(n_tp)])

    def swap_core(array):
        return lax.ppermute(array, "dp", [(i, i ^ 1) for i in range(2 * n_line)])

    def swap_line(array, flip):
        return lax.ppermute(array, "dp", [(i, i ^ (2 * flip)) for i in range(2 * n_line)])

    def hop(array, pairs):
        return lax.ppermute(array, "dp", [(2 * s + c, 2 * d + c) for s, d in pairs for c in (0, 1)])

    def to_neighbours(block):
        return swap_tp(block, 1), swap_tp(block, 2)

    def to_diagonal(block_1, block_2):
        size = block_1.shape[0] // 2
        return swap_tp(block_1[:size], 2), swap_tp(block_2[size:], 1)

    def from_others(array):
        return [swap_tp(array, r) for r in range(1, n_tp)]

    gain, shift, last_bias = (a.reshape(1, features) for a in (norm_gain, norm_bias, out_bias))
    normed, both = norm_rows(tokens, upstream, gain, shift)
    normed_blocks = [normed, *from_others(normed)]
    above_1, below_1 = hop(both, [(0, 1), (1, 2), (2, 3)]), hop(both, [(1, 0), (2, 1), (3, 2)])

    by_owner = jnp.stack([segment_ids.reshape(n_tp, rows), positions.reshape(n_tp, rows)])
    owner = tp_place ^ jnp.arange(n_tp)
    pick = (owner[:, None] == jnp.arange(n_tp)[None, :]).astype(jnp.int32)
    arranged = jnp.sum(pick[None, :, :, None] * by_owner[:, None, :, :], 2).reshape(2, group_rows)
    seg, place = arranged[0], arranged[1]
    cosine_table, sine_table = rotary_tables(place, ROT)
    cosine, sine = cosine_table[:, 0, :], sine_table[:, 0, :]
    still = jnp.zeros((group_rows, HEAD_DIM - ROT), wide)
    quiet = jnp.zeros((group_rows, ROT // 2), wide)
    tables = [
        jnp.concatenate([cosine, still + 1.0], 1),
        jnp.concatenate([-sine[:, : ROT // 2], quiet, still], 1),
        jnp.concatenate([quiet, sine[:, : ROT // 2], still], 1),
    ]
    tables = [jnp.concatenate([t] * (128 // HEAD_DIM), 1) for t in tables]
    parts_weight = qkv_weight.transpose(1, 0, 2)
    parts_bias = qkv_bias.reshape(3, 1, heads_wide)

    normed_blocks, tables, seg, place, late_upstream = tie(normed_blocks, tables, seg, place, upstream)
    upstream_r1, upstream_r2 = to_neighbours(late_upstream)
    group_normed, qkv = project(normed_blocks, parts_weight, parts_bias, tables)

    group_normed, qkv, upstream_r1, upstream_r2, above_1, below_1 = tie(
        group_normed, qkv, upstream_r1, upstream_r2, above_1, below_1
    )
    upstream_r3 = to_diagonal(upstream_r1, upstream_r2)
    above_2, below_2 = hop(above_1, [(1, 2), (2, 3)]), hop(below_1, [(1, 0), (2, 1)])
    slot_1 = jnp.where(line_place % 2 == 1, above_1, below_1)
    upstream_r3, slot_1 = tie(upstream_r3, slot_1)
    slot_1_r1, slot_1_r2 = to_neighbours(slot_1)
    upstream_blocks = [upstream, upstream_r1, upstream_r2, *upstream_r3]
    group_upstream, context, projected_grad, qkv_bias_grad = attention(
        upstream_blocks, qkv, dense_weight, seg, place, tables
    )

    slot_1_r1, slot_1_r2, above_2, below_2, group_upstream, context, projected_grad = tie(
        slot_1_r1, slot_1_r2, above_2, below_2, group_upstream, context, projected_grad
    )
    above_3, below_3 = hop(above_2, [(2, 3)]), hop(below_2, [(1, 0)])
    slot_1_r3 = to_diagonal(slot_1_r1, slot_1_r2)
    slot_2 = jnp.where(line_place >= 2, above_2, below_2)
    pair_part = outer_pair(group_normed, projected_grad, context, group_upstream)

    slot_layout = (
        [(0, 0, rows), (1, 0, rows), (2, 0, rows), (3, 0, rows)],
        [(0, rows, rows), (1, rows, rows), (2, rows, rows), (4, 0, rows)],
    )
    weights = (up_weight, down_weight, up_bias.reshape(1, hidden))
    group_normed, group_upstream, context, projected_grad, pair_part, above_3, below_3, slot_1_r3 = tie(
        group_normed, group_upstream, context, projected_grad, pair_part, above_3, below_3, slot_1_r3
    )
    slot_2_r1, slot_2_r2 = to_neighbours(slot_2)
    pair_share = lax.psum_scatter(pair_part, "dp", scatter_dimension=0, tiled=True)
    layouts = [
        ([(0, 0, group_rows)], [(1, 0, group_rows)]),
        tuple([(i + 2, first, size) for i, first, size in part] for part in slot_layout),
    ]
    group_0, group_1 = feed(
        [group_normed, group_upstream, slot_1, slot_1_r1, slot_1_r2, *slot_1_r3], layouts, *weights
    )

    slot_2_r1, slot_2_r2, group_0, group_1 = tie(slot_2_r1, slot_2_r2, group_0, group_1)
    slot_3 = jnp.where(
        line_place == 0, below_3, jnp.where(line_place == 1, below_1, jnp.where(line_place == 2, above_1, above_3))
    )
    slot_2_r3 = to_diagonal(slot_2_r1, slot_2_r2)
    slot_3_r1, slot_3_r2 = to_neighbours(slot_3)
    active, up_input_grad, up_bias_grad = group_0[2:]
    own_part, *parts = back_to_tokens(
        n_tp, active, context, up_input_grad, projected_grad, down_weight, dense_weight, up_weight, parts_weight
    )

    slot_2_r3, own_part, parts, slot_3_r1, slot_3_r2 = tie(slot_2_r3, own_part, parts, slot_3_r1, slot_3_r2)
    slot_3_r3 = to_diagonal(slot_3_r1, slot_3_r2)
    (group_2,) = feed([slot_2, slot_2_r1, slot_2_r2, *slot_2_r3], [slot_layout], *weights)

    slot_3_r3, parts, group_2 = tie(slot_3_r3, parts, group_2)
    got = [swap_tp(part, r + 1) for r, part in enumerate(parts)]
    (group_3,) = feed([slot_3, slot_3_r1, slot_3_r2, *slot_3_r3], [slot_layout], *weights)

    group_3, pair_share = tie(group_3, pair_share)
    pair_sum = lax.all_gather(pair_share, "dp", axis=0, tiled=True)

    groups = [group_0, group_1, group_2, group_3]
    normeds, upstreams, actives, up_grads = ([g[i] for g in groups] for i in range(4))
    up_part = outer_sum(line_place, normeds, up_grads)
    up_part, actives, upstreams = tie(up_part, list(actives), list(upstreams))
    other_up_part = swap_core(up_part)
    down_part = outer_sum(line_place, actives, upstreams)
    got, own_part, down_part = tie(got, own_part, down_part)
    other_down_part = swap_core(down_part)
    mixed, input_grad, sums = norm_back(tokens, upstream, gain, last_bias, own_part, *got)
    turn = swap_tp(sums, 1)
    up_weight_grad = added(up_part, other_up_part)
    turn, up_weight_grad = tie(turn, up_weight_grad)
    sums = sums + turn
    turn = swap_tp(sums, 2)
    down_weight_grad = added(down_part, other_down_part)
    turn, down_weight_grad, pair_sum = tie(turn, down_weight_grad, pair_sum)
    sums = sums + turn
    small = jnp.concatenate([sums.reshape(1, -1), qkv_bias_grad.reshape(1, -1), up_bias_grad], 1)
    turn = swap_core(small)
    qkv_weight_grad, dense_weight_grad = widen_pair(pair_sum, features)
    qkv_weight_grad = qkv_weight_grad.reshape(3, features, heads_wide).transpose(1, 0, 2)
    turn, qkv_weight_grad = tie(turn, qkv_weight_grad)
    small = small + turn
    turns = [swap_line(small, k) for k in range(1, n_line)]
    small = ((small + turns[0]) + (turns[1] + turns[2]))[0]
    norm_gain_grad = small[:features]
    norm_bias_grad = small[features : 2 * features]
    out_bias_grad = small[2 * features : 3 * features]
    qkv_bias_grad = small[3 * features : 3 * features + 3 * heads_wide].reshape(3, heads_wide)
    up_bias_grad = small[3 * features + 3 * heads_wide :]

    return (
        mixed,
        input_grad,
        norm_gain_grad,
        norm_bias_grad,
        qkv_weight_grad,
        qkv_bias_grad,
        dense_weight_grad,
        up_weight_grad,
        up_bias_grad,
        down_weight_grad,
        out_bias_grad,
    )


def allowed_block(segment_ids, positions, begin_row, block_rows):
    seg_rows = lax.dynamic_slice_in_dim(segment_ids, begin_row, block_rows)
    place_rows = lax.dynamic_slice_in_dim(positions, begin_row, block_rows)
    return (seg_rows[:, None] == segment_ids[None, :]) & (positions[None, :] <= place_rows[:, None])


def block_scores(query_block, keys_low, allowed):
    scores = (
        jnp.einsum("qhe,khe->hqk", query_block, keys_low, preferred_element_type=jnp.float32)
        * 0.125
    )
    return jnp.where(allowed[None], scores, masked_score)


def up_projection(gathered, up_weight, up_bias):
    up_input = jnp.dot(gathered, up_weight, preferred_element_type=jnp.float32) + up_bias.astype(
        jnp.float32
    )
    return (up_input, jax.nn.gelu(up_input, approximate=True).astype(jnp.bfloat16))


def row_product(left, right):
    return jnp.dot(left, right, preferred_element_type=jnp.float32)


def general_shards(
    tokens,
    upstream,
    segment_ids,
    positions,
    norm_gain,
    norm_bias,
    qkv_weight,
    qkv_bias,
    dense_weight,
    up_weight,
    up_bias,
    down_weight,
    out_bias,
):
    head_count = qkv_weight.shape[2] // HEAD_DIM
    inputs = tokens.astype(jnp.float32)
    normed_low = layer_norm(inputs, norm_gain, norm_bias).astype(jnp.bfloat16)
    gathered = lax.all_gather(normed_low, "tp", axis=0, tiled=True)
    group_rows = gathered.shape[0]
    block_rows = math.gcd(group_rows, 512)
    block_count = group_rows // block_rows
    projected = (
        jnp.einsum("td,dch->tch", gathered, qkv_weight, preferred_element_type=jnp.float32)
        + qkv_bias.astype(jnp.float32)[None]
    )
    head_shape = (group_rows, head_count, HEAD_DIM)
    cosine_table, sine_table = rotary_tables(positions, ROT)
    queries = rotate(projected[:, 0].reshape(head_shape), cosine_table, sine_table).astype(
        jnp.bfloat16
    )
    keys_low = rotate(projected[:, 1].reshape(head_shape), cosine_table, sine_table).astype(
        jnp.bfloat16
    )
    values_low = projected[:, 2].reshape(head_shape).astype(jnp.bfloat16)

    def forward_block(block_index):
        begin_row = block_index * block_rows
        query_block = lax.dynamic_slice_in_dim(queries, begin_row, block_rows, 0)
        scores = block_scores(
            query_block, keys_low, allowed_block(segment_ids, positions, begin_row, block_rows)
        )
        highest_score = jnp.max(scores, -1, keepdims=True)
        exponent = jnp.exp(scores - highest_score)
        totals = jnp.sum(exponent, -1, keepdims=True)
        soft_low = (exponent / totals).astype(jnp.bfloat16)
        context_block = jnp.einsum(
            "hqk,khe->qhe", soft_low, values_low, preferred_element_type=jnp.float32
        )
        return (context_block.astype(jnp.bfloat16), highest_score + jnp.log(totals))

    context_blocks, log_blocks = lax.map(forward_block, jnp.arange(block_count, dtype=jnp.int32))
    context_low = context_blocks.reshape(group_rows, head_count * HEAD_DIM)
    up_input, up_active_low = up_projection(gathered, up_weight, up_bias)
    summed = lax.psum_scatter(
        row_product(context_low, dense_weight) + row_product(up_active_low, down_weight),
        "tp",
        scatter_dimension=0,
        tiled=True,
    )
    mixed = (inputs + summed + out_bias).astype(jnp.bfloat16)
    upstream_all = lax.all_gather(upstream, "tp", axis=0, tiled=True)
    unit_column = jnp.ones((group_rows,), jnp.bfloat16)
    out_bias_grad = jnp.einsum(
        "t,td->d", unit_column, upstream_all, preferred_element_type=jnp.float32
    )
    dense_weight_grad = jnp.einsum(
        "te,td->ed", context_low, upstream_all, preferred_element_type=jnp.float32
    )
    down_weight_grad = jnp.einsum(
        "tf,td->fd", up_active_low, upstream_all, preferred_element_type=jnp.float32
    )
    context_grad = jnp.einsum(
        "td,ed->te", upstream_all, dense_weight, preferred_element_type=jnp.float32
    )
    context_grad_low = context_grad.astype(jnp.bfloat16).reshape(head_shape)
    active_grad = jnp.einsum(
        "td,fd->tf", upstream_all, down_weight, preferred_element_type=jnp.float32
    )
    _, gelu_back = jax.vjp(partial(jax.nn.gelu, approximate=True), up_input)
    up_input_grad = gelu_back(active_grad)[0].astype(jnp.bfloat16)
    up_bias_grad = jnp.einsum(
        "t,tf->f", unit_column, up_input_grad, preferred_element_type=jnp.float32
    )

    def backward_block(running, block_index):
        key_grad, value_grad = running
        begin_row = block_index * block_rows
        query_block = lax.dynamic_slice_in_dim(queries, begin_row, block_rows, 0)
        output_grad = lax.dynamic_slice_in_dim(context_grad_low, begin_row, block_rows, 0)
        log_totals = lax.dynamic_index_in_dim(log_blocks, block_index, 0, keepdims=False)
        scores = block_scores(
            query_block, keys_low, allowed_block(segment_ids, positions, begin_row, block_rows)
        )
        attn_soft = jnp.exp(scores - log_totals)
        value_grad = value_grad + jnp.einsum(
            "hqk,qhe->khe",
            attn_soft.astype(jnp.bfloat16),
            output_grad,
            preferred_element_type=jnp.float32,
        )
        prob_grad = jnp.einsum(
            "qhe,khe->hqk", output_grad, values_low, preferred_element_type=jnp.float32
        )
        row_dots = jnp.sum(attn_soft * prob_grad, -1, keepdims=True)
        score_grad = (attn_soft * (prob_grad - row_dots)).astype(jnp.bfloat16)
        query_grad = (
            jnp.einsum("hqk,khe->qhe", score_grad, keys_low, preferred_element_type=jnp.float32)
            * 0.125
        )
        key_grad = (
            key_grad
            + jnp.einsum(
                "hqk,qhe->khe", score_grad, query_block, preferred_element_type=jnp.float32
            )
            * 0.125
        )
        return ((key_grad, value_grad), query_grad)

    empty_grad = jnp.zeros(head_shape, jnp.float32)
    (key_grad, value_grad), query_blocks = lax.scan(
        backward_block, (empty_grad, empty_grad), jnp.arange(block_count, dtype=jnp.int32)
    )
    query_grad = query_blocks.reshape(head_shape)
    projected_grad = jnp.stack(
        [
            rotate(query_grad, cosine_table, -sine_table),
            rotate(key_grad, cosine_table, -sine_table),
            value_grad,
        ],
        axis=1,
    )
    projected_grad = projected_grad.reshape(group_rows, 3, head_count * HEAD_DIM).astype(
        jnp.bfloat16
    )
    qkv_bias_grad = jnp.einsum(
        "t,tch->ch", unit_column, projected_grad, preferred_element_type=jnp.float32
    )
    qkv_weight_grad = jnp.einsum(
        "td,tch->dch", gathered, projected_grad, preferred_element_type=jnp.float32
    )
    up_weight_grad = jnp.einsum(
        "td,tf->df", gathered, up_input_grad, preferred_element_type=jnp.float32
    )
    first = jnp.einsum(
        "tch,dch->td", projected_grad, qkv_weight, preferred_element_type=jnp.float32
    )
    normed_grad = lax.psum_scatter(
        first
        + jnp.einsum("tf,df->td", up_input_grad, up_weight, preferred_element_type=jnp.float32),
        "tp",
        scatter_dimension=0,
        tiled=True,
    )
    _, norm_back = jax.vjp(layer_norm, inputs, norm_gain, norm_bias)
    input_part, gain_part, shift_part = norm_back(normed_grad)
    input_grad = upstream.astype(jnp.float32) + input_part
    norm_gain_grad, norm_bias_grad = lax.psum((gain_part, shift_part), ("dp", "tp"))
    (
        qkv_weight_grad,
        qkv_bias_grad,
        dense_weight_grad,
        up_weight_grad,
        up_bias_grad,
        down_weight_grad,
        out_bias_grad,
    ) = lax.psum(
        (
            qkv_weight_grad,
            qkv_bias_grad,
            dense_weight_grad,
            up_weight_grad,
            up_bias_grad,
            down_weight_grad,
            out_bias_grad,
        ),
        "dp",
    )
    return (
        mixed,
        input_grad,
        norm_gain_grad,
        norm_bias_grad,
        qkv_weight_grad,
        qkv_bias_grad,
        dense_weight_grad,
        up_weight_grad,
        up_bias_grad,
        down_weight_grad,
        out_bias_grad,
    )


def solution(mesh):
    fits = mesh.shape["dp"] == 8 and mesh.shape["tp"] == 4
    return jax.shard_map(
        shards if fits else general_shards,
        mesh=mesh,
        in_specs=(
            P(("dp", "tp"), None),
            P(("dp", "tp"), None),
            P("dp"),
            P("dp"),
            P(),
            P(),
            P(None, None, "tp"),
            P(None, "tp"),
            P("tp", None),
            P(None, "tp"),
            P("tp"),
            P("tp", None),
            P(),
        ),
        out_specs=(
            P(("dp", "tp"), None),
            P(("dp", "tp"), None),
            P(),
            P(),
            P(None, None, "tp"),
            P(None, "tp"),
            P("tp", None),
            P(None, "tp"),
            P("tp"),
            P("tp", None),
            P(),
        ),
        check_vma=False,
    )
```

```python
from functools import partial
import math

import jax
import jax.numpy as jnp
from jax import lax
from jax.experimental import pallas as pl
from jax.experimental.pallas import tpu as pltpu
from jax.sharding import PartitionSpec as P

HEAD_DIM = 64
ROT = 32
norm_epsilon = 1e-05
masked_score = -1e30
low = jnp.bfloat16
wide = jnp.float32
VMEM = 56 * 2**20
HASTE = 0.02
LANES = 256


def dot(left, right, left_dim, right_dim, kind=wide):
    return lax.dot_general(
        left, right, (((left_dim,), (right_dim,)), ((), ())), preferred_element_type=wide
    ).astype(kind)


def layer_norm(values, gain, shift):
    averaged = jnp.mean(values, -1, keepdims=True)
    centred = values - averaged
    spread = jnp.mean(centred * centred, -1, keepdims=True)
    return centred * lax.rsqrt(spread + norm_epsilon) * gain + shift


def rotary_tables(places, rot_dims):
    half_rot = rot_dims // 2
    frequency = jnp.power(10000.0, -2.0 * jnp.arange(half_rot).astype(wide) / rot_dims)
    phases = places.astype(wide)[:, None] * frequency[None, :]
    cosine_table = jnp.concatenate([jnp.cos(phases), jnp.cos(phases)], -1)[:, None, :]
    sine_table = jnp.concatenate([jnp.sin(phases), jnp.sin(phases)], -1)[:, None, :]
    return (cosine_table, sine_table)


def rotate(values, cosine_table, sine_table):
    rot_dims = cosine_table.shape[-1]
    half_rot = rot_dims // 2
    rotated_part = values[..., :rot_dims]
    turned = jnp.concatenate([-rotated_part[..., half_rot:], rotated_part[..., :half_rot]], -1)
    return jnp.concatenate(
        [rotated_part * cosine_table + turned * sine_table, values[..., rot_dims:]], -1
    )


def gelu_and_slope(v):
    square = v * v
    inner = jnp.tanh(v * (0.7978845608 + 0.035677408137 * square))
    half = 0.5 + 0.5 * inner
    slope = half + (v - v * (inner * inner)) * (0.3989422804 + 0.0535161122 * square)
    return v * half, slope


def kernel_call(body, flops, out_shape, traffic=0, **kinds):
    return pl.pallas_call(
        body,
        out_shape=out_shape,
        compiler_params=pltpu.CompilerParams(vmem_limit_bytes=VMEM),
        cost_estimate=pl.CostEstimate(
            flops=int(flops * HASTE), bytes_accessed=traffic + int(flops * HASTE) // 512, transcendentals=0
        ),
        **kinds,
    )


def sds(shape, kind):
    return jax.ShapeDtypeStruct(shape, kind)


def whole_block(array):
    zeros = (0,) * array.ndim
    return pl.BlockSpec(array.shape, lambda *_: zeros, pipeline_mode=pl.Buffered(1))


def fixed_block(shape):
    zeros = (0,) * len(shape)
    return pl.BlockSpec(shape, lambda *_: zeros)


def assemble(target, pieces):
    at = 0
    for ref, first, size in pieces:
        target[at : at + size, :] = ref[first : first + size, :]
        at += size


def turned(values, cosine, sine_low, sine_high):
    return (
        values * cosine
        + pltpu.roll(values, 128 - ROT // 2, 1) * sine_low
        + pltpu.roll(values, ROT // 2, 1) * sine_high
    )


def row_means(inputs):
    centred = inputs - jnp.mean(inputs, -1, keepdims=True)
    spread = jnp.mean(centred * centred, -1, keepdims=True)
    scale = lax.rsqrt(spread + norm_epsilon)
    return centred * scale, scale


def norm_kernel(tokens, upstream, gain, shift, normed, both):
    unit, _ = row_means(tokens[...].astype(wide))
    rows = tokens.shape[0]
    normed[...] = (unit * gain[...] + shift[...]).astype(low)
    both[:rows, :] = normed[...]
    both[rows:, :] = upstream[...]


def norm_rows(tokens, upstream, gain, shift):
    rows, features = tokens.shape
    arrays = [tokens, upstream, gain, shift]
    return kernel_call(
        norm_kernel,
        rows * features * 512,
        [sds((rows, features), low), sds((2 * rows, features), low)],
        grid=(1,),
        in_specs=[whole_block(a) for a in arrays],
        out_specs=[fixed_block((rows, features)), fixed_block((2 * rows, features))],
    )(*arrays)


def norm_back_kernel(tokens, upstream, gain, out_bias, own, got_1, got_2, got_3, mixed, input_grad, sums):
    rows = tokens.shape[0]
    inputs, cotangent = tokens[...].astype(wide), upstream[...].astype(wide)

    def total(first):
        span = slice(first, first + rows)
        return (own[span, :] + got_1[span, :].astype(wide)) + (
            got_2[span, :].astype(wide) + got_3[span, :].astype(wide)
        )

    mixed[...] = (inputs + total(0) + out_bias[...]).astype(low)
    unit, scale = row_means(inputs)
    normed_grad = total(rows)
    e = normed_grad * gain[...]
    along = jnp.mean(e * unit, -1, keepdims=True)
    input_grad[...] = cotangent + (e - jnp.mean(e, -1, keepdims=True) - unit * along) * scale
    sums[0:1, :] = jnp.sum(normed_grad * unit, 0, keepdims=True)
    sums[1:2, :] = jnp.sum(normed_grad, 0, keepdims=True)
    sums[2:3, :] = jnp.sum(cotangent, 0, keepdims=True)


def norm_back(*arrays):
    rows, features = arrays[0].shape
    shapes = [(rows, features), (rows, features), (3, features)]
    return kernel_call(
        norm_back_kernel,
        rows * features * 1024,
        [sds(s, k) for s, k in zip(shapes, (low, wide, wide))],
        grid=(1,),
        in_specs=[whole_block(a) for a in arrays],
        out_specs=[fixed_block(s) for s in shapes],
    )(*arrays)


def project_kernel(count, *refs):
    weight, bias, cosine, sine_low, sine_high, rows_out, out = refs[count:]
    part = pl.program_id(0)

    @pl.when(part == 0)
    def _():
        assemble(rows_out, [(r, 0, r.shape[0]) for r in refs[:count]])

    projected = dot(rows_out[...], weight[0], 1, 0) + bias[0].astype(wide)

    @pl.when(part < 2)
    def _():
        scale = jnp.where(part == 0, 0.125, 1.0)
        for j in range(0, projected.shape[1], 128):
            rotated = turned(projected[:, j : j + 128], cosine[...], sine_low[...], sine_high[...])
            out[0, :, j : j + 128] = (rotated * scale).astype(low)

    @pl.when(part == 2)
    def _():
        out[0] = projected.astype(low)


def project(blocks, weight, bias, tables):
    tokens = sum(b.shape[0] for b in blocks)
    _, features, width = weight.shape
    table = whole_block(tables[0])
    return kernel_call(
        partial(project_kernel, len(blocks)),
        6 * tokens * features * width,
        [sds((tokens, features), low), sds((3, tokens, width), low)],
        grid=(3,),
        in_specs=[whole_block(a) for a in blocks]
        + [
            pl.BlockSpec((1, features, width), lambda c: (c, 0, 0)),
            pl.BlockSpec((1, 1, width), lambda c: (c, 0, 0)),
            table,
            table,
            table,
        ],
        out_specs=[fixed_block((tokens, features)), pl.BlockSpec((1, tokens, width), lambda c: (c, 0, 0))],
    )(*blocks, weight, bias, *tables)


def attention_kernel(count, *refs):
    (queries, keys, values, dense, mask, cosine, sine_low, sine_high) = refs[count:-4]
    rows_out, context, out, bias_out = refs[-4:]

    @pl.when(pl.program_id(0) == 0)
    def _():
        assemble(rows_out, [(r, 0, r.shape[0]) for r in refs[:count]])

    q, k, v = queries[0], keys[0], values[0]
    g = dot(rows_out[...], dense[...], 1, 1, low)
    lane = lax.broadcasted_iota(jnp.int32, q.shape, 1) // HEAD_DIM
    found = []
    for head in range(q.shape[1] // HEAD_DIM):
        mine = lane == head
        scores = dot(jnp.where(mine, q, jnp.zeros_like(q)), k, 1, 1) + mask[...]
        exponent = jnp.exp(scores - jnp.max(scores, -1, keepdims=True))
        soft = exponent * (1.0 / jnp.sum(exponent, -1, keepdims=True))
        soft_low = soft.astype(low)
        prob_grad = dot(jnp.where(mine, g, jnp.zeros_like(g)), v, 1, 1)
        row_dots = jnp.sum(soft * prob_grad, -1, keepdims=True)
        score_grad = (soft * (prob_grad - row_dots)).astype(low)
        found.append(
            (dot(soft_low, v, 1, 0), dot(score_grad, k, 1, 0), dot(score_grad, q, 0, 0), dot(soft_low, g, 0, 0))
        )
    parts = []
    for of_heads in zip(*found):
        chosen = of_heads[0]
        for head, value in enumerate(of_heads[1:], 1):
            chosen = jnp.where(lane == head, value, chosen)
        parts.append(chosen)
    context[...] = parts[0].astype(low)
    back = (cosine[...], -sine_low[...], -sine_high[...])
    turn_back = lambda value: jnp.concatenate(
        [turned(value[:, j : j + 128], *back) for j in range(0, value.shape[1], 128)], 1
    )
    grads = [turn_back(parts[1] * 0.125), turn_back(parts[2]), parts[3]]
    for c, value in enumerate(grads):
        rounded = value.astype(low)
        out[c] = rounded
        bias_out[c] = jnp.sum(rounded.astype(wide), 0, keepdims=True)


def attention(blocks, qkv, dense_weight, mask, tables, lanes=LANES):
    _, tokens, width = qkv.shape
    features = dense_weight.shape[1]
    extras = [mask, *tables]
    part = lambda c: pl.BlockSpec((1, tokens, lanes), lambda j: (c, 0, j))
    return kernel_call(
        partial(attention_kernel, len(blocks)),
        20 * tokens * tokens * width,
        [
            sds((tokens, features), low),
            sds((tokens, width), low),
            sds((3, tokens, width), low),
            sds((3, 1, width), wide),
        ],
        grid=(width // lanes,),
        in_specs=[whole_block(b) for b in blocks]
        + [part(0), part(1), part(2), pl.BlockSpec((lanes, features), lambda j: (j, 0))]
        + [whole_block(e) for e in extras],
        out_specs=[
            fixed_block((tokens, features)),
            pl.BlockSpec((tokens, lanes), lambda j: (0, j)),
            pl.BlockSpec((3, tokens, lanes), lambda j: (0, 0, j)),
            pl.BlockSpec((3, 1, lanes), lambda j: (0, 0, j)),
        ],
    )(*blocks, qkv, qkv, qkv, dense_weight, *extras)


def outer_pair_kernel(left, right, context, upstream, out):
    count = right.shape[0]
    for c in range(count):
        out[c] = dot(left[...], right[c], 0, 0, low)
    out[count] = dot(context[...], upstream[...], 0, 0, low)


def outer_pair(left, right, context, upstream):
    count, tokens, width = right.shape
    features = left.shape[1]
    columns = pl.BlockSpec((tokens, width), lambda i: (0, i))
    found = kernel_call(
        outer_pair_kernel,
        2 * (count + 1) * tokens * features * width,
        sds((count + 1, features, width), low),
        grid=(features // width,),
        in_specs=[columns, whole_block(right), whole_block(context), columns],
        out_specs=pl.BlockSpec((count + 1, width, width), lambda i: (0, i, 0)),
    )(left, right, context, upstream)
    return found.reshape((count + 1) * features, width)


def widen_pair_kernel(n_first, given, first, second):
    step = pl.program_id(0)

    @pl.when(step < n_first)
    def _():
        first[...] = given[...].astype(wide)

    @pl.when(step >= n_first)
    def _():
        width = given.shape[1]
        for i in range(given.shape[0] // width):
            second[:, i * width : (i + 1) * width] = given[i * width : (i + 1) * width, :].astype(wide)


def widen_pair(given, features, tile=1024):
    rows, width = given.shape
    each = features // tile
    n_first = rows // tile - each
    return kernel_call(
        partial(widen_pair_kernel, n_first),
        rows * width * 256,
        [sds((rows - features, width), wide), sds((width, features), wide)],
        6 * rows * width,
        grid=(n_first + each,),
        in_specs=[pl.BlockSpec((tile, width), lambda s: (s, 0))],
        out_specs=[
            pl.BlockSpec((tile, width), lambda s: (jnp.minimum(s, n_first - 1), 0)),
            pl.BlockSpec((width, tile), lambda s: (0, jnp.maximum(s - n_first, 0))),
        ],
    )(given)


def feed_kernel(layouts, n_arrays, *refs):
    arrays, refs = refs[:n_arrays], refs[n_arrays:]
    up_weight, down_weight, up_bias = refs[:3]
    outs = refs[3:]
    pick = lambda layout: [(arrays[i], first, size) for i, first, size in layout]

    @pl.when(pl.program_id(0) == 0)
    def _():
        for (normed_layout, upstream_layout), (normed_out, upstream_out, *_) in zip(layouts, fives(outs)):
            assemble(normed_out, pick(normed_layout))
            assemble(upstream_out, pick(upstream_layout))

    bias = up_bias[...].astype(wide)
    for normed_out, upstream_out, active_out, grad_out, sum_out in fives(outs):
        active, slope = gelu_and_slope(dot(normed_out[...], up_weight[...], 1, 0) + bias)
        active_out[...] = active.astype(low)
        rounded = (dot(upstream_out[...], down_weight[...], 1, 1) * slope).astype(low)
        grad_out[...] = rounded
        sum_out[...] = jnp.sum(rounded.astype(wide), 0, keepdims=True)


def fives(outs):
    return [outs[i : i + 5] for i in range(0, len(outs), 5)]


def feed(arrays, layouts, up_weight, down_weight, up_bias, tile=512):
    features, hidden = up_weight.shape
    tokens = sum(size for _, _, size in layouts[0][0])
    rows_spec = fixed_block((tokens, features))
    tile_spec = pl.BlockSpec((tokens, tile), lambda j: (0, j))
    sum_spec = pl.BlockSpec((1, tile), lambda j: (0, j))
    shapes = [sds((tokens, features), low)] * 2 + [sds((tokens, hidden), low)] * 2 + [sds((1, hidden), wide)]
    found = kernel_call(
        partial(feed_kernel, layouts, len(arrays)),
        4 * len(layouts) * tokens * features * hidden,
        shapes * len(layouts),
        grid=(hidden // tile,),
        in_specs=[whole_block(a) for a in arrays]
        + [
            pl.BlockSpec((features, tile), lambda j: (0, j)),
            pl.BlockSpec((tile, features), lambda j: (j, 0)),
            pl.BlockSpec((1, tile), lambda j: (0, j)),
        ],
        out_specs=[rows_spec, rows_spec, tile_spec, tile_spec, sum_spec] * len(layouts),
    )(*arrays, up_weight, down_weight, up_bias)
    return fives(found)


def back_kernel(n_tp, active, context, up_grad, part_grad, down, dense, up, part_weight, own, *sent):
    rows = active.shape[0] // n_tp
    mixed = dot(active[...], down[...], 1, 0) + dot(context[...], dense[...], 1, 0)
    normed_grad = dot(up_grad[...], up[...], 1, 1)
    for c in range(3):
        normed_grad = normed_grad + dot(part_grad[c], part_weight[c], 1, 1)
    for i, value in enumerate((mixed, normed_grad)):
        span = slice(i * rows, (i + 1) * rows)
        own[span, :] = value[:rows]
        for r in range(1, n_tp):
            sent[r - 1][span, :] = value[r * rows : (r + 1) * rows].astype(low)


def back_to_tokens(n_tp, active, context, up_grad, part_grad, down, dense, up, part_weight, tile=512):
    tokens, hidden = active.shape
    features, width = down.shape[1], context.shape[1]
    rows = 2 * tokens // n_tp
    column = pl.BlockSpec((rows, tile), lambda j: (0, j))
    return kernel_call(
        partial(back_kernel, n_tp),
        4 * tokens * features * (hidden + 2 * width),
        [sds((rows, features), wide)] + [sds((rows, features), low)] * (n_tp - 1),
        grid=(features // tile,),
        in_specs=[whole_block(a) for a in (active, context, up_grad, part_grad)]
        + [
            pl.BlockSpec((hidden, tile), lambda j: (0, j)),
            pl.BlockSpec((width, tile), lambda j: (0, j)),
            pl.BlockSpec((tile, hidden), lambda j: (j, 0)),
            pl.BlockSpec((3, tile, width), lambda j: (0, j, 0)),
        ],
        out_specs=[column] * n_tp,
    )(active, context, up_grad, part_grad, down, dense, up, part_weight)


def outer_kernel(count, place, *refs):
    out = refs[2 * count]
    for here in range(count):

        @pl.when(place[0] == here)
        def _():
            total = None
            for there in range(count):
                i = here ^ there
                term = dot(refs[i][...], refs[count + i][...], 0, 0)
                total = term if total is None else total + term
            out[...] = total.astype(out.dtype)


def outer_sum(place, lefts, rights, tile_m=512, tile_n=1024):
    count, (tokens, m), n = len(lefts), lefts[0].shape, rights[0].shape[1]
    return kernel_call(
        partial(outer_kernel, count),
        2 * count * tokens * m * n,
        sds((m, n), low),
        grid_spec=pltpu.PrefetchScalarGridSpec(
            num_scalar_prefetch=1,
            grid=(n // tile_n, m // tile_m),
            in_specs=[pl.BlockSpec((tokens, tile_m), lambda j, i, _: (0, i))] * count
            + [pl.BlockSpec((tokens, tile_n), lambda j, i, _: (0, j))] * count,
            out_specs=pl.BlockSpec((tile_m, tile_n), lambda j, i, _: (i, j)),
        ),
    )(place.reshape(1).astype(jnp.int32), *lefts, *rights)


def add_kernel(*refs):
    total = refs[0][...].astype(wide)
    for ref in refs[1:-1]:
        total = total + ref[...].astype(wide)
    refs[-1][...] = total


def added(*terms, tile=512):
    m, n = terms[0].shape
    spec = pl.BlockSpec((tile, n), lambda i: (i, 0))
    return kernel_call(
        add_kernel, m * n * 256, sds((m, n), wide), 8 * m * n, grid=(m // tile,), in_specs=[spec] * len(terms), out_specs=spec
    )(*terms)


def tie(*arrays):
    return lax.optimization_barrier(arrays)


def shards(
    tokens,
    upstream,
    segment_ids,
    positions,
    norm_gain,
    norm_bias,
    qkv_weight,
    qkv_bias,
    dense_weight,
    up_weight,
    up_bias,
    down_weight,
    out_bias,
):
    n_tp, n_line = 4, 4
    dp_place, tp_place = lax.axis_index("dp"), lax.axis_index("tp")
    line_place = dp_place // 2
    rows, features = tokens.shape
    group_rows = rows * n_tp
    heads_wide = qkv_weight.shape[2]
    hidden = up_weight.shape[1]

    def swap_tp(array, flip):
        return lax.ppermute(array, "tp", [(i, i ^ flip) for i in range(n_tp)])

    def swap_core(array):
        return lax.ppermute(array, "dp", [(i, i ^ 1) for i in range(2 * n_line)])

    def swap_line(array, flip):
        return lax.ppermute(array, "dp", [(i, i ^ (2 * flip)) for i in range(2 * n_line)])

    def hop(array, pairs):
        return lax.ppermute(array, "dp", [(2 * s + c, 2 * d + c) for s, d in pairs for c in (0, 1)])

    def to_neighbours(block):
        return swap_tp(block, 1), swap_tp(block, 2)

    def to_diagonal(block_1, block_2):
        size = block_1.shape[0] // 2
        return swap_tp(block_1[:size], 2), swap_tp(block_2[size:], 1)

    def from_others(array):
        return [swap_tp(array, r) for r in range(1, n_tp)]

    gain, shift, last_bias = (a.reshape(1, features) for a in (norm_gain, norm_bias, out_bias))
    normed, both = norm_rows(tokens, upstream, gain, shift)
    normed_blocks = [normed, *from_others(normed)]
    above_1, below_1 = hop(both, [(0, 1), (1, 2), (2, 3)]), hop(both, [(1, 0), (2, 1), (3, 2)])

    by_owner = jnp.stack([segment_ids.reshape(n_tp, rows), positions.reshape(n_tp, rows)])
    owner = tp_place ^ jnp.arange(n_tp)
    pick = (owner[:, None] == jnp.arange(n_tp)[None, :]).astype(jnp.int32)
    arranged = jnp.sum(pick[None, :, :, None] * by_owner[:, None, :, :], 2).reshape(2, group_rows)
    seg, place = arranged[0], arranged[1]
    cosine_table, sine_table = rotary_tables(place, ROT)
    cosine, sine = cosine_table[:, 0, :], sine_table[:, 0, :]
    still = jnp.zeros((group_rows, HEAD_DIM - ROT), wide)
    quiet = jnp.zeros((group_rows, ROT // 2), wide)
    tables = [
        jnp.concatenate([cosine, still + 1.0], 1),
        jnp.concatenate([-sine[:, : ROT // 2], quiet, still], 1),
        jnp.concatenate([quiet, sine[:, : ROT // 2], still], 1),
    ]
    tables = [jnp.concatenate([t] * (128 // HEAD_DIM), 1) for t in tables]
    parts_weight = qkv_weight.transpose(1, 0, 2)
    parts_bias = qkv_bias.reshape(3, 1, heads_wide)

    allowed = (seg[:, None] == seg[None, :]) & (place[None, :] <= place[:, None])
    mask = jnp.where(allowed, 0.0, masked_score).astype(wide)
    normed_blocks, tables, mask, late_upstream = tie(normed_blocks, tables, mask, upstream)
    upstream_r1, upstream_r2 = to_neighbours(late_upstream)
    group_normed, qkv = project(normed_blocks, parts_weight, parts_bias, tables)

    group_normed, qkv, upstream_r1, upstream_r2, above_1, below_1 = tie(
        group_normed, qkv, upstream_r1, upstream_r2, above_1, below_1
    )
    upstream_r3 = to_diagonal(upstream_r1, upstream_r2)
    above_2, below_2 = hop(above_1, [(1, 2), (2, 3)]), hop(below_1, [(1, 0), (2, 1)])
    slot_1 = jnp.where(line_place % 2 == 1, above_1, below_1)
    upstream_r3, slot_1 = tie(upstream_r3, slot_1)
    slot_1_r1, slot_1_r2 = to_neighbours(slot_1)
    upstream_blocks = [upstream, upstream_r1, upstream_r2, *upstream_r3]
    group_upstream, context, projected_grad, qkv_bias_grad = attention(
        upstream_blocks, qkv, dense_weight, mask, tables
    )

    slot_1_r1, slot_1_r2, above_2, below_2, group_upstream, context, projected_grad = tie(
        slot_1_r1, slot_1_r2, above_2, below_2, group_upstream, context, projected_grad
    )
    above_3, below_3 = hop(above_2, [(2, 3)]), hop(below_2, [(1, 0)])
    slot_1_r3 = to_diagonal(slot_1_r1, slot_1_r2)
    slot_2 = jnp.where(line_place >= 2, above_2, below_2)
    pair_part = outer_pair(group_normed, projected_grad, context, group_upstream)

    slot_layout = (
        [(0, 0, rows), (1, 0, rows), (2, 0, rows), (3, 0, rows)],
        [(0, rows, rows), (1, rows, rows), (2, rows, rows), (4, 0, rows)],
    )
    weights = (up_weight, down_weight, up_bias.reshape(1, hidden))
    group_normed, group_upstream, context, projected_grad, pair_part, above_3, below_3, slot_1_r3 = tie(
        group_normed, group_upstream, context, projected_grad, pair_part, above_3, below_3, slot_1_r3
    )
    slot_2_r1, slot_2_r2 = to_neighbours(slot_2)
    pair_share = lax.psum_scatter(pair_part, "dp", scatter_dimension=0, tiled=True)
    layouts = [
        ([(0, 0, group_rows)], [(1, 0, group_rows)]),
        tuple([(i + 2, first, size) for i, first, size in part] for part in slot_layout),
    ]
    group_0, group_1 = feed(
        [group_normed, group_upstream, slot_1, slot_1_r1, slot_1_r2, *slot_1_r3], layouts, *weights
    )

    slot_2_r1, slot_2_r2, group_0, group_1 = tie(slot_2_r1, slot_2_r2, group_0, group_1)
    slot_3 = jnp.where(
        line_place == 0, below_3, jnp.where(line_place == 1, below_1, jnp.where(line_place == 2, above_1, above_3))
    )
    slot_2_r3 = to_diagonal(slot_2_r1, slot_2_r2)
    slot_3_r1, slot_3_r2 = to_neighbours(slot_3)
    active, up_input_grad, up_bias_grad = group_0[2:]
    own_part, *parts = back_to_tokens(
        n_tp, active, context, up_input_grad, projected_grad, down_weight, dense_weight, up_weight, parts_weight
    )

    slot_2_r3, own_part, parts, slot_3_r1, slot_3_r2 = tie(slot_2_r3, own_part, parts, slot_3_r1, slot_3_r2)
    slot_3_r3 = to_diagonal(slot_3_r1, slot_3_r2)
    (group_2,) = feed([slot_2, slot_2_r1, slot_2_r2, *slot_2_r3], [slot_layout], *weights)

    slot_3_r3, parts, group_2 = tie(slot_3_r3, parts, group_2)
    got = [swap_tp(part, r + 1) for r, part in enumerate(parts)]
    (group_3,) = feed([slot_3, slot_3_r1, slot_3_r2, *slot_3_r3], [slot_layout], *weights)

    group_3, pair_share = tie(group_3, pair_share)
    pair_sum = lax.all_gather(pair_share, "dp", axis=0, tiled=True)

    groups = [group_0, group_1, group_2, group_3]
    normeds, upstreams, actives, up_grads = ([g[i] for g in groups] for i in range(4))
    up_part = outer_sum(line_place, normeds, up_grads)
    up_part, actives, upstreams = tie(up_part, list(actives), list(upstreams))
    other_up_part = swap_core(up_part)
    down_part = outer_sum(line_place, actives, upstreams)
    got, own_part, down_part = tie(got, own_part, down_part)
    other_down_part = swap_core(down_part)
    mixed, input_grad, sums = norm_back(tokens, upstream, gain, last_bias, own_part, *got)
    turn = swap_tp(sums, 1)
    up_weight_grad = added(up_part, other_up_part)
    turn, up_weight_grad = tie(turn, up_weight_grad)
    sums = sums + turn
    turn = swap_tp(sums, 2)
    down_weight_grad = added(down_part, other_down_part)
    turn, down_weight_grad, pair_sum = tie(turn, down_weight_grad, pair_sum)
    sums = sums + turn
    small = jnp.concatenate([sums.reshape(1, -1), qkv_bias_grad.reshape(1, -1), up_bias_grad], 1)
    turn = swap_core(small)
    qkv_weight_grad, dense_weight_grad = widen_pair(pair_sum, features)
    qkv_weight_grad = qkv_weight_grad.reshape(3, features, heads_wide).transpose(1, 0, 2)
    turn, qkv_weight_grad = tie(turn, qkv_weight_grad)
    small = small + turn
    turns = [swap_line(small, k) for k in range(1, n_line)]
    small = ((small + turns[0]) + (turns[1] + turns[2]))[0]
    norm_gain_grad = small[:features]
    norm_bias_grad = small[features : 2 * features]
    out_bias_grad = small[2 * features : 3 * features]
    qkv_bias_grad = small[3 * features : 3 * features + 3 * heads_wide].reshape(3, heads_wide)
    up_bias_grad = small[3 * features + 3 * heads_wide :]

    return (
        mixed,
        input_grad,
        norm_gain_grad,
        norm_bias_grad,
        qkv_weight_grad,
        qkv_bias_grad,
        dense_weight_grad,
        up_weight_grad,
        up_bias_grad,
        down_weight_grad,
        out_bias_grad,
    )


def allowed_block(segment_ids, positions, begin_row, block_rows):
    seg_rows = lax.dynamic_slice_in_dim(segment_ids, begin_row, block_rows)
    place_rows = lax.dynamic_slice_in_dim(positions, begin_row, block_rows)
    return (seg_rows[:, None] == segment_ids[None, :]) & (positions[None, :] <= place_rows[:, None])


def block_scores(query_block, keys_low, allowed):
    scores = (
        jnp.einsum("qhe,khe->hqk", query_block, keys_low, preferred_element_type=jnp.float32)
        * 0.125
    )
    return jnp.where(allowed[None], scores, masked_score)


def up_projection(gathered, up_weight, up_bias):
    up_input = jnp.dot(gathered, up_weight, preferred_element_type=jnp.float32) + up_bias.astype(
        jnp.float32
    )
    return (up_input, jax.nn.gelu(up_input, approximate=True).astype(jnp.bfloat16))


def row_product(left, right):
    return jnp.dot(left, right, preferred_element_type=jnp.float32)


def general_shards(
    tokens,
    upstream,
    segment_ids,
    positions,
    norm_gain,
    norm_bias,
    qkv_weight,
    qkv_bias,
    dense_weight,
    up_weight,
    up_bias,
    down_weight,
    out_bias,
):
    head_count = qkv_weight.shape[2] // HEAD_DIM
    inputs = tokens.astype(jnp.float32)
    normed_low = layer_norm(inputs, norm_gain, norm_bias).astype(jnp.bfloat16)
    gathered = lax.all_gather(normed_low, "tp", axis=0, tiled=True)
    group_rows = gathered.shape[0]
    block_rows = math.gcd(group_rows, 512)
    block_count = group_rows // block_rows
    projected = (
        jnp.einsum("td,dch->tch", gathered, qkv_weight, preferred_element_type=jnp.float32)
        + qkv_bias.astype(jnp.float32)[None]
    )
    head_shape = (group_rows, head_count, HEAD_DIM)
    cosine_table, sine_table = rotary_tables(positions, ROT)
    queries = rotate(projected[:, 0].reshape(head_shape), cosine_table, sine_table).astype(
        jnp.bfloat16
    )
    keys_low = rotate(projected[:, 1].reshape(head_shape), cosine_table, sine_table).astype(
        jnp.bfloat16
    )
    values_low = projected[:, 2].reshape(head_shape).astype(jnp.bfloat16)

    def forward_block(block_index):
        begin_row = block_index * block_rows
        query_block = lax.dynamic_slice_in_dim(queries, begin_row, block_rows, 0)
        scores = block_scores(
            query_block, keys_low, allowed_block(segment_ids, positions, begin_row, block_rows)
        )
        highest_score = jnp.max(scores, -1, keepdims=True)
        exponent = jnp.exp(scores - highest_score)
        totals = jnp.sum(exponent, -1, keepdims=True)
        soft_low = (exponent / totals).astype(jnp.bfloat16)
        context_block = jnp.einsum(
            "hqk,khe->qhe", soft_low, values_low, preferred_element_type=jnp.float32
        )
        return (context_block.astype(jnp.bfloat16), highest_score + jnp.log(totals))

    context_blocks, log_blocks = lax.map(forward_block, jnp.arange(block_count, dtype=jnp.int32))
    context_low = context_blocks.reshape(group_rows, head_count * HEAD_DIM)
    up_input, up_active_low = up_projection(gathered, up_weight, up_bias)
    summed = lax.psum_scatter(
        row_product(context_low, dense_weight) + row_product(up_active_low, down_weight),
        "tp",
        scatter_dimension=0,
        tiled=True,
    )
    mixed = (inputs + summed + out_bias).astype(jnp.bfloat16)
    upstream_all = lax.all_gather(upstream, "tp", axis=0, tiled=True)
    unit_column = jnp.ones((group_rows,), jnp.bfloat16)
    out_bias_grad = jnp.einsum(
        "t,td->d", unit_column, upstream_all, preferred_element_type=jnp.float32
    )
    dense_weight_grad = jnp.einsum(
        "te,td->ed", context_low, upstream_all, preferred_element_type=jnp.float32
    )
    down_weight_grad = jnp.einsum(
        "tf,td->fd", up_active_low, upstream_all, preferred_element_type=jnp.float32
    )
    context_grad = jnp.einsum(
        "td,ed->te", upstream_all, dense_weight, preferred_element_type=jnp.float32
    )
    context_grad_low = context_grad.astype(jnp.bfloat16).reshape(head_shape)
    active_grad = jnp.einsum(
        "td,fd->tf", upstream_all, down_weight, preferred_element_type=jnp.float32
    )
    _, gelu_back = jax.vjp(partial(jax.nn.gelu, approximate=True), up_input)
    up_input_grad = gelu_back(active_grad)[0].astype(jnp.bfloat16)
    up_bias_grad = jnp.einsum(
        "t,tf->f", unit_column, up_input_grad, preferred_element_type=jnp.float32
    )

    def backward_block(running, block_index):
        key_grad, value_grad = running
        begin_row = block_index * block_rows
        query_block = lax.dynamic_slice_in_dim(queries, begin_row, block_rows, 0)
        output_grad = lax.dynamic_slice_in_dim(context_grad_low, begin_row, block_rows, 0)
        log_totals = lax.dynamic_index_in_dim(log_blocks, block_index, 0, keepdims=False)
        scores = block_scores(
            query_block, keys_low, allowed_block(segment_ids, positions, begin_row, block_rows)
        )
        attn_soft = jnp.exp(scores - log_totals)
        value_grad = value_grad + jnp.einsum(
            "hqk,qhe->khe",
            attn_soft.astype(jnp.bfloat16),
            output_grad,
            preferred_element_type=jnp.float32,
        )
        prob_grad = jnp.einsum(
            "qhe,khe->hqk", output_grad, values_low, preferred_element_type=jnp.float32
        )
        row_dots = jnp.sum(attn_soft * prob_grad, -1, keepdims=True)
        score_grad = (attn_soft * (prob_grad - row_dots)).astype(jnp.bfloat16)
        query_grad = (
            jnp.einsum("hqk,khe->qhe", score_grad, keys_low, preferred_element_type=jnp.float32)
            * 0.125
        )
        key_grad = (
            key_grad
            + jnp.einsum(
                "hqk,qhe->khe", score_grad, query_block, preferred_element_type=jnp.float32
            )
            * 0.125
        )
        return ((key_grad, value_grad), query_grad)

    empty_grad = jnp.zeros(head_shape, jnp.float32)
    (key_grad, value_grad), query_blocks = lax.scan(
        backward_block, (empty_grad, empty_grad), jnp.arange(block_count, dtype=jnp.int32)
    )
    query_grad = query_blocks.reshape(head_shape)
    projected_grad = jnp.stack(
        [
            rotate(query_grad, cosine_table, -sine_table),
            rotate(key_grad, cosine_table, -sine_table),
            value_grad,
        ],
        axis=1,
    )
    projected_grad = projected_grad.reshape(group_rows, 3, head_count * HEAD_DIM).astype(
        jnp.bfloat16
    )
    qkv_bias_grad = jnp.einsum(
        "t,tch->ch", unit_column, projected_grad, preferred_element_type=jnp.float32
    )
    qkv_weight_grad = jnp.einsum(
        "td,tch->dch", gathered, projected_grad, preferred_element_type=jnp.float32
    )
    up_weight_grad = jnp.einsum(
        "td,tf->df", gathered, up_input_grad, preferred_element_type=jnp.float32
    )
    first = jnp.einsum(
        "tch,dch->td", projected_grad, qkv_weight, preferred_element_type=jnp.float32
    )
    normed_grad = lax.psum_scatter(
        first
        + jnp.einsum("tf,df->td", up_input_grad, up_weight, preferred_element_type=jnp.float32),
        "tp",
        scatter_dimension=0,
        tiled=True,
    )
    _, norm_back = jax.vjp(layer_norm, inputs, norm_gain, norm_bias)
    input_part, gain_part, shift_part = norm_back(normed_grad)
    input_grad = upstream.astype(jnp.float32) + input_part
    norm_gain_grad, norm_bias_grad = lax.psum((gain_part, shift_part), ("dp", "tp"))
    (
        qkv_weight_grad,
        qkv_bias_grad,
        dense_weight_grad,
        up_weight_grad,
        up_bias_grad,
        down_weight_grad,
        out_bias_grad,
    ) = lax.psum(
        (
            qkv_weight_grad,
            qkv_bias_grad,
            dense_weight_grad,
            up_weight_grad,
            up_bias_grad,
            down_weight_grad,
            out_bias_grad,
        ),
        "dp",
    )
    return (
        mixed,
        input_grad,
        norm_gain_grad,
        norm_bias_grad,
        qkv_weight_grad,
        qkv_bias_grad,
        dense_weight_grad,
        up_weight_grad,
        up_bias_grad,
        down_weight_grad,
        out_bias_grad,
    )


def solution(mesh):
    fits = mesh.shape["dp"] == 8 and mesh.shape["tp"] == 4
    return jax.shard_map(
        shards if fits else general_shards,
        mesh=mesh,
        in_specs=(
            P(("dp", "tp"), None),
            P(("dp", "tp"), None),
            P("dp"),
            P("dp"),
            P(),
            P(),
            P(None, None, "tp"),
            P(None, "tp"),
            P("tp", None),
            P(None, "tp"),
            P("tp"),
            P("tp", None),
            P(),
        ),
        out_specs=(
            P(("dp", "tp"), None),
            P(("dp", "tp"), None),
            P(),
            P(),
            P(None, None, "tp"),
            P(None, "tp"),
            P("tp", None),
            P(None, "tp"),
            P("tp"),
            P("tp", None),
            P(),
        ),
        check_vma=False,
    )
```
